256 devices in a mesh: context: 32 (over z, y_lo, core), tensor: 8 (over y_hi, x).
Axes of the slice: x: 4, y: 4 (y_hi: 2, y_lo: 2; y = y_hi * 2 + y_lo), z: 8, core: 2. Of those that a mesh axis runs over, the one named last changes fastest.
Arguments:
- layer_input: bfloat16 [4096, 8192], P(('context', 'tensor')), may hold values from -24 to 24
- query_stream: bfloat16 [4096, 4096], P('context', 'tensor'), may hold values from -6 to 6
- key_stream: bfloat16 [4096, 4096], P('context', 'tensor'), may hold values from -6 to 6
- value_stream: bfloat16 [4096, 4096], P('context', 'tensor'), may hold values from -6 to 6
- output_grad: bfloat16 [4096, 4096], P('context', 'tensor'), may hold values from -6 to 6
- filter_taps: bfloat16 [4096, 128], P('tensor'), may hold values from -0.5 to 0.5
- skip_gain: float32 [4096], P('tensor'), may hold values from 0.5 to 1.5
- value_weight: bfloat16 [8192, 4096], P(None, 'tensor'), may hold values from -0.0625 to 0.0625
Outputs:
- query_grad: bfloat16 [4096, 4096], P('context', 'tensor')
- key_grad: bfloat16 [4096, 4096], P('context', 'tensor')
- value_grad: bfloat16 [4096, 4096], P('context', 'tensor')
- filter_grad: float32 [4096, 128], P('tensor')
- skip_grad: float32 [4096], P('tensor')
- input_grad: bfloat16 [4096, 8192], P(('context', 'tensor'))
- weight_grad: float32 [8192, 4096], P('context', 'tensor')
The draws below stay inside these ranges and needn't reach their ends.
All inputs are finite; a program needn't handle non-finite values.
Results may differ from the reference program's by a relative error of at most 0.015.
Values may be sent and summed in bfloat16 or wider, within the bound.
A program may use at most 128 MiB of HBM per device.

```python
import jax
import jax.numpy as jnp
from jax import lax

D = 8192
TAPS = 128
CH = 4096
TOKENS = 4096
N_TENSOR = 8


def with_spikes(array, rng, source, target, parts, factor):
    def block_of(position):
        return (jnp.arange(array.shape[position]) // (array.shape[position] // parts)).reshape((-1,) + (1,) * (array.ndim - 1 - position))

    one_side = jax.random.permutation(rng, parts)[block_of(target)]
    second = (block_of(target) + parts // 2) % parts
    return jnp.where((block_of(source) == one_side) | (block_of(source) == second), factor * array, array)


def shard_levels(stream_key, extent, pieces, smallest, largest):
    def one(position, blocks):
        heights = jax.random.uniform(jax.random.fold_in(jax.random.fold_in(stream_key, 6), position), (blocks,), jnp.float32, smallest / len(pieces), largest / len(pieces))
        return jnp.repeat(jnp.exp(heights), extent[position] // blocks).reshape((-1,) + (1,) * (len(extent) - position - 1))

    level = one(*pieces[0])
    for cut in pieces[1:]:
        level = level * one(*cut)
    return level


def scatter_about(key, shape, spread, limit, pieces=(), kind=jnp.bfloat16):
    drawn = jax.random.normal(key, shape, jnp.float32) * spread
    if len(pieces) > 0:
        drawn = shard_levels(key, shape, pieces, -0.22, 0.18) * drawn
    return jnp.clip(drawn, min=-limit, max=limit).astype(kind)


def noise_with(rng, dims, spread, reach, shards, heavy, kind=jnp.bfloat16):
    values = spread * jax.random.normal(rng, dims, jnp.float32)
    if shards:
        values = values * shard_levels(rng, dims, shards, -0.22, 0.18)
    return jnp.clip(with_spikes(values, jax.random.fold_in(rng, 3), *heavy), -reach, reach).astype(kind)


def setup_inputs(seed: int = 0) -> dict:
    seeds = jax.random.split(jax.random.key(seed), 9)
    return {
        "layer_input": noise_with(seeds[0], (TOKENS, D), 1.0, 24.0, ((0, 256),), (0, 1, 256, 6.0)),
        "query_stream": scatter_about(seeds[1], (TOKENS, CH), 1.0, 6.0, ((0, 32), (1, 8))),
        "key_stream": scatter_about(seeds[2], (TOKENS, CH), 1.0, 6.0, ((0, 32), (1, 8))),
        "value_stream": scatter_about(seeds[3], (TOKENS, CH), 1.0, 6.0, ((0, 32), (1, 8))),
        "output_grad": scatter_about(seeds[4], (TOKENS, CH), 1.0, 6.0, ((0, 32), (1, 8))),
        "filter_taps": scatter_about(seeds[5], (CH, TAPS), TAPS ** -0.5, 0.5, ((0, 8),)),
        "skip_gain": jnp.clip(0.5 + 1.0 * jax.random.uniform(seeds[6], (CH,), jnp.float32) ** shard_levels(seeds[6], (CH,), ((0, 8),), -0.2, 0.2), 0.5, 1.5),
        "value_weight": scatter_about(seeds[7], (D, CH), D ** -0.5, 0.0625, ((1, 8),)),
    }


def causal_filter(inner32, taps32):
    padded = jnp.concatenate([jnp.zeros((TAPS - 1, CH), jnp.float32), inner32], axis=0)

    def add_tap(j, total):
        piece = lax.dynamic_slice_in_dim(padded, (TAPS - 1 - j).astype(jnp.int32), TOKENS, 0)
        return total + piece * taps32[:, j]

    return lax.fori_loop(jnp.int32(0), jnp.int32(TAPS), add_tap, jnp.zeros((TOKENS, CH), jnp.float32))


def anti_filter(delta32, taps32):
    padded = jnp.concatenate([delta32, jnp.zeros((TAPS - 1, CH), jnp.float32)], axis=0)

    def add_tap(j, total):
        piece = lax.dynamic_slice_in_dim(padded, j.astype(jnp.int32), TOKENS, 0)
        return total + piece * taps32[:, j]

    return lax.fori_loop(jnp.int32(0), jnp.int32(TAPS), add_tap, jnp.zeros((TOKENS, CH), jnp.float32))


def taps_gradient(delta32, inner32):
    padded = jnp.concatenate([jnp.zeros((TAPS - 1, CH), jnp.float32), inner32], axis=0)

    def one_tap(j):
        piece = lax.dynamic_slice_in_dim(padded, (TAPS - 1 - j).astype(jnp.int32), TOKENS, 0)
        return jnp.sum(delta32 * piece, axis=0)

    return lax.map(one_tap, jnp.arange(TAPS, dtype=jnp.int32)).T


def reference(layer_input, query_stream, key_stream, value_stream, output_grad, filter_taps, skip_gain, value_weight):
    taps32 = filter_taps.astype(jnp.float32)
    inner = (key_stream.astype(jnp.float32) * value_stream.astype(jnp.float32)).astype(jnp.bfloat16)
    inner32 = inner.astype(jnp.float32)
    mixed = causal_filter(inner32, taps32) + skip_gain[None, :] * inner32
    query_grad = (output_grad.astype(jnp.float32) * mixed).astype(jnp.bfloat16)
    delta = (output_grad.astype(jnp.float32) * query_stream.astype(jnp.float32)).astype(jnp.bfloat16)
    delta32 = delta.astype(jnp.float32)
    back = anti_filter(delta32, taps32) + skip_gain[None, :] * delta32
    key_grad = (back * value_stream.astype(jnp.float32)).astype(jnp.bfloat16)
    value_grad = (back * key_stream.astype(jnp.float32)).astype(jnp.bfloat16)
    filter_grad = taps_gradient(delta32, inner32)
    skip_grad = jnp.sum(delta32 * inner32, axis=0)
    group = CH // N_TENSOR
    summed = jnp.zeros((TOKENS, D), jnp.float32)
    for index in range(N_TENSOR):
        grads_part = value_grad[:, index * group:(index + 1) * group]
        weight_part = value_weight[:, index * group:(index + 1) * group]
        term = jnp.dot(grads_part, weight_part.T, preferred_element_type=jnp.float32).astype(jnp.bfloat16)
        term = lax.optimization_barrier(term)
        summed = summed + term.astype(jnp.float32)
    input_grad = summed.astype(jnp.bfloat16)
    weight_grad = jnp.dot(layer_input.T, value_grad, preferred_element_type=jnp.float32)
    return query_grad, key_grad, value_grad, filter_grad, skip_grad, input_grad, weight_grad
```

```python
import functools

import jax
import jax.numpy as jnp
from jax import lax
from jax.experimental import pallas as pl
from jax.experimental.pallas import tpu as pltpu
from jax.sharding import PartitionSpec as P

MESH = pl.DeviceIdType.MESH
BF16 = jnp.bfloat16
F32 = jnp.float32

NZ, NYL, NCORE, NYH, NX = 8, 2, 2, 2, 4
NQ = NZ * NYL
NT = NYH * NX
TAPS = 128
ROWS = 128
CH = 512
SUB = 16
D = 8192
WIDE = D // NQ
CHUNKS = 4
CCOLS = D // CHUNKS


def kernel(
    x_hbm, q_hbm, k_hbm, v_hbm, g_hbm, taps_hbm, gain_hbm, w_hbm,
    qg_hbm, kg_hbm, vg_hbm, fg_hbm, sg_hbm, ig_hbm, wg_hbm,
    qv, kv, vv, gv, taps_v, gain_v, w_v,
    inner, delta, halo_d, halo_i, tapst, dext, iext, d8, e8, back,
    qgv, kgv, xa, ga, tpart, trecv, ig, wacc, wrecv, wout,
    fpart, fcore, fsum, frs, ffull, fgt, sgv,
    in_sems, out_sems, halo_s, halo_r, a2a_s, a2a_r, ag_s, ag_r, b_s, b_r, c_s, c_r,
    core_s, core_r, rs_s, rs_r, fa_s, fa_r,
):
    con = lax.axis_index("context")
    ten = lax.axis_index("tensor")
    z, yl, core = con // 4, (con // 2) % 2, con % 2
    yh, x = ten // 4, ten % 4
    q = con // 2

    def at(zz, yy, cc):
        return (zz % NZ) * 4 + (yy % 2) * 2 + cc % 2

    def ten_at(hh, xx):
        return (hh % 2) * 4 + xx % 4

    def remote(src, dst, ss, rs, device):
        return pltpu.make_async_remote_copy(
            src_ref=src, dst_ref=dst, send_sem=ss, recv_sem=rs, device_id=device, device_id_type=MESH
        )

    loads = [
        pltpu.make_async_copy(src, dst, in_sems.at[i])
        for i, (src, dst) in enumerate(
            [(k_hbm, kv), (v_hbm, vv), (g_hbm, gv), (q_hbm, qv), (taps_hbm, taps_v), (gain_hbm, gain_v), (w_hbm, w_v)]
        )
    ]
    for copy in loads:
        copy.start()

    barrier = pltpu.get_barrier_semaphore()
    above = (con + 1) % 32
    below = (con + 31) % 32

    def greet(device):
        pl.semaphore_signal(barrier, inc=1, device_id=device, device_id_type=MESH)

    greet((above, ten))
    greet((below, ten))
    greet((at(z, yl, core + 1), ten))

    def greet_q(i, carry):
        greet((at(z + i // 2, yl + i % 2, core), ten))
        return carry

    lax.fori_loop(1, NQ, greet_q, 0)

    def greet_t(i, carry):
        greet((con, (ten + i) % NT))
        return carry

    lax.fori_loop(1, NT, greet_t, 0)

    loads[0].wait()
    loads[1].wait()
    loads[2].wait()
    loads[3].wait()
    inner[...] = (kv[...].astype(F32) * vv[...].astype(F32)).astype(BF16)
    delta[...] = (gv[...].astype(F32) * qv[...].astype(F32)).astype(BF16)
    dext[pl.ds(0, ROWS), :] = delta[...].astype(F32)
    iext[pl.ds(ROWS, ROWS), :] = inner[...].astype(F32)

    pl.semaphore_wait(barrier, 3 + (NQ - 1) + (NT - 1))

    halo_delta = remote(delta, halo_d, halo_s.at[0], halo_r.at[0], (below, ten))
    halo_inner = remote(inner, halo_i, halo_s.at[1], halo_r.at[1], (above, ten))
    halo_delta.start()
    halo_inner.start()

    own_x = pltpu.make_async_copy(
        x_hbm.at[:, pl.ds(pl.multiple_of(q * WIDE, WIDE), WIDE)], xa.at[q, ten], in_sems.at[7]
    )
    own_x.start()

    def a2a_copy(i):
        dest = ((z + i // 2) % NZ) * 2 + (yl + i % 2) % 2
        return remote(
            x_hbm.at[:, pl.ds(pl.multiple_of(dest * WIDE, WIDE), WIDE)],
            xa.at[q, ten],
            a2a_s.at[i],
            a2a_r.at[i],
            (dest * 2 + core, ten),
        )

    def a2a_start(i, carry):
        a2a_copy(i).start()
        return carry

    lax.fori_loop(1, NQ, a2a_start, 0)

    loads[4].wait()
    loads[5].wait()
    tapst[...] = taps_v[...].astype(F32).T

    halo_delta.wait_recv()
    keep_d = jnp.where(con == 31, 0.0, 1.0).astype(F32)
    dext[pl.ds(ROWS, ROWS), :] = halo_d[...].astype(F32) * keep_d
    for r in range(8):
        d8[r, pl.ds(0, 248), :] = dext[pl.ds(r, 248), :]

    def lanes(l):
        return pl.ds(pl.multiple_of(l * 128, 128), 128)

    def back_tile(l, carry):
        cols = lanes(l)

        acc = gain_v[:, cols] * d8[0, pl.ds(0, ROWS), cols]
        for r in range(8):
            for a in range(16):
                acc = acc + tapst[pl.ds(8 * a + r, 1), cols] * d8[r, pl.ds(8 * a, ROWS), cols]
        back[:, cols] = acc
        return carry

    lax.fori_loop(0, 4, back_tile, 0)

    backs = back[...]
    kgv[...] = (backs * vv[...].astype(F32)).astype(BF16)
    ga[q] = (backs * kv[...].astype(F32)).astype(BF16)

    def slot(zz, rel):
        return (zz % NZ) * 2 + (yl + rel) % 2

    def b_copy(index, where, device):
        return remote(ga.at[where], ga.at[where], b_s.at[index], b_r.at[index], (device, ten))

    up, down = at(z + 1, yl, core), at(z + 7, yl, core)

    def right(d, rel):
        return b_copy(1 + (d - 1) * 4 + rel, slot(z + 9 - d, rel), up)

    def left(d, rel):
        return b_copy(1 + (d - 1) * 4 + 2 + rel, slot(z + d - 1, rel), down)

    def arrived_right(d, rel):
        b_copy(1 + (d - 1) * 4 + rel, slot(z + 8 - d, rel), up).wait_recv()

    def arrived_left(d, rel):
        b_copy(1 + (d - 1) * 4 + 2 + rel, slot(z + d, rel), down).wait_recv()

    right(1, 0).start()
    left(1, 0).start()
    across = b_copy(0, slot(z, 0), at(z, yl + 1, core))
    across.start()

    out_copies = [
        pltpu.make_async_copy(kgv, kg_hbm, out_sems.at[0]),
        pltpu.make_async_copy(ga.at[q], vg_hbm, out_sems.at[1]),
    ]
    for copy in out_copies:
        copy.start()

    own_x.wait()

    def a2a_wait(i, carry):
        source = ((z + NZ - i // 2) % NZ) * 2 + (yl + i % 2) % 2
        remote(xa.at[source, ten], xa.at[source, ten], a2a_s.at[i], a2a_r.at[i], (source * 2 + core, ten)).wait_recv()
        return carry

    lax.fori_loop(1, NQ, a2a_wait, 0)

    def ag_copy(index, part, half, device):
        ref = xa.at[:, part] if half is None else xa.at[pl.ds(8 * half, 8), part]
        return remote(ref, ref, ag_s.at[index], ag_r.at[index], (con, device))

    x_up, x_down = ten_at(yh, x + 1), ten_at(yh, x + 3)
    other = ten_at(yh + 1, x)
    ag_y = ag_copy(0, ten, None, other)
    ag_y.start()
    ag_copy(1, ten, None, x_up).start()
    ag_copy(2, ten, None, x_down).start()

    loads[6].wait()

    def c_copy(i, chunk):
        cols = pl.ds(chunk * CCOLS, CCOLS)
        index = i * CHUNKS + chunk
        return remote(
            tpart.at[(ten + i) % NT, :, cols], trecv.at[i, :, cols], c_s.at[index], c_r.at[index], (con, (ten + i) % NT)
        )

    def terms(chunk):
        def part(n, carry):
            cols = pl.ds(pl.multiple_of(chunk * CCOLS + n * 512, 512), 512)
            product = lax.dot_general(ga[q], w_v[cols, :], (((1,), (1,)), ((), ())), preferred_element_type=F32)
            tpart[:, :, cols] = product.astype(BF16).reshape(NT, SUB, 512)
            return carry

        lax.fori_loop(0, CCOLS // 512, part, 0)

        def send(i, carry):
            c_copy(i, chunk).start()
            return carry

        lax.fori_loop(1, NT, send, 0)

    terms(0)
    terms(1)
    across.wait_recv()
    right(1, 1).start()
    left(1, 1).start()
    terms(2)
    terms(3)

    def filter_tile(l, carry):
        cols = lanes(l)

        for r in range(8):
            for a in range(16):
                product = iext[pl.ds(ROWS, ROWS), cols] * d8[r, pl.ds(8 * a, ROWS), cols]
                fpart[pl.ds(8 * a + r, 1), cols] = jnp.sum(product, axis=0, keepdims=True)
        return carry

    def forward(d, rel):
        arrived_right(d, rel)
        if d < 3 or rel == 0:
            right(d + 1, rel).start()
        arrived_left(d, rel)
        if d < 3 or rel == 1:
            left(d + 1, rel).start()

    lax.fori_loop(0, 2, filter_tile, 0)
    forward(1, 0)
    ag_y.wait_recv()
    ag_copy(3, other, None, x_up).start()
    ag_copy(4, other, None, x_down).start()
    lax.fori_loop(2, 4, filter_tile, 0)
    forward(1, 1)

    half = CH // 2
    mine = pl.ds(pl.multiple_of(core * half, half), half)
    theirs = pl.ds(pl.multiple_of((1 - core) * half, half), half)
    partner = (at(z, yl, core + 1), ten)
    f_core = remote(fpart.at[:, theirs], fcore, core_s.at[0], core_r.at[0], partner)
    f_core.start()

    ag_copy(1, x_down, None, x_up).wait_recv()
    ag_copy(5, x_down, 0, x_up).start()
    ag_copy(2, x_up, None, x_down).wait_recv()
    ag_copy(6, x_up, 1, x_down).start()

    halo_inner.wait_recv()
    keep_i = jnp.where(con == 0, 0.0, 1.0).astype(F32)
    iext[pl.ds(0, ROWS), :] = halo_i[...].astype(F32) * keep_i
    e8[0] = iext[...]
    for r in range(1, 8):
        e8[r, pl.ds(0, 248), :] = iext[pl.ds(r, 248), :]

    f_core.wait_recv()
    fsum[...] = fpart[:, mine] + fcore[...]

    def rs_copy(i):
        dest = ((z + i // 2) % NZ) * 2 + (yl + i % 2) % 2
        return remote(
            fsum.at[pl.ds(pl.multiple_of(dest * 8, 8), 8), :], frs.at[i], rs_s.at[i], rs_r.at[i], (dest * 2 + core, ten)
        )

    def rs_start(i, carry):
        rs_copy(i).start()
        return carry

    lax.fori_loop(1, NQ, rs_start, 0)

    def mixed_tile(l, carry):
        cols = lanes(l)
        acc = iext[pl.ds(ROWS, ROWS), cols] * gain_v[:, cols]
        for r in range(8):
            for b in range(17):
                if 0 <= TAPS - 8 * b - r < TAPS:
                    acc = acc + tapst[pl.ds(TAPS - 8 * b - r, 1), cols] * e8[r, pl.ds(8 * b, ROWS), cols]
        qgv[:, cols] = (gv[:, cols].astype(F32) * acc).astype(BF16)
        return carry

    lax.fori_loop(0, 2, mixed_tile, 0)
    forward(2, 0)
    lax.fori_loop(2, 4, mixed_tile, 0)
    forward(2, 1)
    copy = pltpu.make_async_copy(qgv, qg_hbm, out_sems.at[2])
    copy.start()
    out_copies.append(copy)

    def rs_wait(i, carry):
        rs_copy(i).wait_recv()
        return carry

    lax.fori_loop(1, NQ, rs_wait, 0)
    total = fsum[pl.ds(pl.multiple_of(q * 8, 8), 8), :]
    for i in range(1, NQ):
        total = total + frs[i]
    my_rows = pl.ds(pl.multiple_of(q * 8, 8), 8)
    ffull[my_rows, mine] = total

    def fa_copy(i, source):
        dest = ((z + i // 2) % NZ) * 2 + (yl + i % 2) % 2
        ref = ffull.at[pl.ds(pl.multiple_of(source * 8, 8), 8), mine]
        return remote(ref, ref, fa_s.at[i], fa_r.at[i], (dest * 2 + core, ten))

    def fa_start(i, carry):
        fa_copy(i, q).start()
        return carry

    lax.fori_loop(1, NQ, fa_start, 0)

    other_down, other_up = ten_at(yh + 1, x + 3), ten_at(yh + 1, x + 1)
    ag_copy(3, other_down, None, x_up).wait_recv()
    ag_copy(7, other_down, 0, x_up).start()
    ag_copy(4, other_up, None, x_down).wait_recv()
    ag_copy(8, other_up, 1, x_down).start()

    forward(3, 0)
    forward(3, 1)

    def fa_wait(i, carry):
        source = ((z + NZ - i // 2) % NZ) * 2 + (yl + i % 2) % 2
        fa_copy(i, source).wait_recv()
        return carry

    lax.fori_loop(1, NQ, fa_wait, 0)
    f_back = remote(ffull.at[:, mine], ffull.at[:, mine], core_s.at[1], core_r.at[1], partner)
    f_back.start()

    arrived_right(4, 0)
    arrived_left(4, 1)

    def product(part, first):
        def rows(m, carry):
            cols = pl.ds(pl.multiple_of(m * 256, 256), 256)
            lhs = xa[:, part, :, cols].reshape(NQ * SUB, 256)
            rhs = ga[:, pl.ds(pl.multiple_of(part * SUB, SUB), SUB), :].reshape(NQ * SUB, CH)
            new = lax.dot_general(lhs, rhs, (((0,), (0,)), ((), ())), preferred_element_type=F32)
            if first:
                wacc[cols, :] = new
            else:
                wacc[cols, :] += new
            return carry

        lax.fori_loop(0, 2, rows, 0)

    product(ten, True)
    product(x_up, False)
    product(x_down, False)
    product(other, False)
    product(other_up, False)
    product(other_down, False)

    f_back_wait = remote(ffull.at[:, theirs], ffull.at[:, theirs], core_s.at[1], core_r.at[1], partner)
    f_back_wait.wait_recv()
    fgt[...] = ffull[...].T
    sgv[...] = ffull[pl.ds(0, 1), :]
    for copy in (
        pltpu.make_async_copy(fgt, fg_hbm, out_sems.at[3]),
        pltpu.make_async_copy(sgv, sg_hbm, out_sems.at[4]),
    ):
        copy.start()
        out_copies.append(copy)

    far, other_far = ten_at(yh, x + 2), ten_at(yh + 1, x + 2)
    ag_copy(5, far, 0, x_up).wait_recv()
    ag_copy(6, far, 1, x_down).wait_recv()
    product(far, False)
    ag_copy(7, other_far, 0, x_up).wait_recv()
    ag_copy(8, other_far, 1, x_down).wait_recv()
    product(other_far, False)
    own_rows = pl.ds(pl.multiple_of(core * 256, 256), 256)
    partner_rows = pl.ds(pl.multiple_of((1 - core) * 256, 256), 256)
    w_core = remote(wacc.at[partner_rows, :], wrecv, core_s.at[2], core_r.at[2], partner)
    w_core.start()

    for chunk in range(CHUNKS):
        for i in range(1, NT):
            c_copy(i, chunk).wait_recv()
        cols = pl.ds(chunk * CCOLS, CCOLS)
        acc = tpart[ten, :, cols].astype(F32)
        for i in range(1, NT):
            acc = acc + trecv[i, :, cols].astype(F32)
        ig[:, cols] = acc.astype(BF16)
    copy = pltpu.make_async_copy(ig, ig_hbm, out_sems.at[5])
    copy.start()
    out_copies.append(copy)

    w_core.wait_recv()
    wout[...] = wacc[own_rows, :] + wrecv[...]
    copy = pltpu.make_async_copy(wout, wg_hbm, out_sems.at[6])
    copy.start()
    out_copies.append(copy)

    halo_delta.wait_send()
    halo_inner.wait_send()

    def sent(i, carry):
        a2a_copy(i).wait_send()
        rs_copy(i).wait_send()
        fa_copy(i, q).wait_send()
        return carry

    lax.fori_loop(1, NQ, sent, 0)
    for index in range(9):
        ag_copy(index, ten, None if index < 5 else 0, x_up).wait_send()
    for index in range(15):
        b_copy(index if index < 14 else 16, slot(z, 0), up).wait_send()

    def c_sent(i, carry):
        for chunk in range(CHUNKS):
            c_copy(i, chunk).wait_send()
        return carry

    lax.fori_loop(1, NT, c_sent, 0)
    f_core.wait_send()
    f_back.wait_send()
    w_core.wait_send()
    for copy in out_copies:
        copy.wait()


def local(layer_input, query_stream, key_stream, value_stream, output_grad, filter_taps, skip_gain, value_weight):
    shape = jax.ShapeDtypeStruct
    vm = pltpu.VMEM
    dma = pltpu.SemaphoreType.DMA
    outs = pl.pallas_call(
        kernel,
        out_shape=(
            shape((ROWS, CH), BF16),
            shape((ROWS, CH), BF16),
            shape((ROWS, CH), BF16),
            shape((CH, TAPS), F32),
            shape((1, CH), F32),
            shape((SUB, D), BF16),
            shape((256, CH), F32),
        ),
        in_specs=[pl.BlockSpec(memory_space=pl.ANY)] * 8,
        out_specs=[pl.BlockSpec(memory_space=pl.ANY)] * 7,
        scratch_shapes=[
            vm((ROWS, CH), BF16),
            vm((ROWS, CH), BF16),
            vm((ROWS, CH), BF16),
            vm((ROWS, CH), BF16),
            vm((CH, TAPS), BF16),
            vm((1, CH), F32),
            vm((D, CH), BF16),
            vm((ROWS, CH), BF16),
            vm((ROWS, CH), BF16),
            vm((ROWS, CH), BF16),
            vm((ROWS, CH), BF16),
            vm((TAPS, CH), F32),
            vm((2 * ROWS, CH), F32),
            vm((2 * ROWS, CH), F32),
            vm((8, 2 * ROWS, CH), F32),
            vm((8, 2 * ROWS, CH), F32),
            vm((ROWS, CH), F32),
            vm((ROWS, CH), BF16),
            vm((ROWS, CH), BF16),
            vm((NQ, NT, SUB, WIDE), BF16),
            vm((NQ, ROWS, CH), BF16),
            vm((NT, SUB, D), BF16),
            vm((NT, SUB, D), BF16),
            vm((SUB, D), BF16),
            vm((WIDE, CH), F32),
            vm((256, CH), F32),
            vm((256, CH), F32),
            vm((TAPS, CH), F32),
            vm((TAPS, CH // 2), F32),
            vm((TAPS, CH // 2), F32),
            vm((NQ, 8, CH // 2), F32),
            vm((TAPS, CH), F32),
            vm((CH, TAPS), F32),
            vm((1, CH), F32),
            dma((8,)),
            dma((7,)),
            dma((2,)), dma((2,)),
            dma((NQ,)), dma((NQ,)),
            dma((9,)), dma((9,)),
            dma((17,)), dma((17,)),
            dma((NT * CHUNKS,)), dma((NT * CHUNKS,)),
            dma((3,)), dma((3,)),
            dma((NQ,)), dma((NQ,)),
            dma((NQ,)), dma((NQ,)),
        ],
        compiler_params=pltpu.CompilerParams(
            collective_id=0, has_side_effects=True, vmem_limit_bytes=52 << 20
        ),
        name="hyena_back",
    )(
        layer_input, query_stream, key_stream, value_stream, output_grad, filter_taps,
        skip_gain.reshape(1, CH), value_weight,
    )
    query_grad, key_grad, value_grad, filter_grad, skip_grad, input_grad, weight_grad = outs
    return (query_grad, key_grad, value_grad, filter_grad, skip_grad.reshape(CH), input_grad, weight_grad)


def solution(mesh):
    placed = (
        P(("context", "tensor"), None),
        P("context", "tensor"),
        P("context", "tensor"),
        P("context", "tensor"),
        P("context", "tensor"),
        P("tensor", None),
        P("tensor"),
        P(None, "tensor"),
    )
    return jax.shard_map(
        local,
        mesh=mesh,
        in_specs=placed,
        out_specs=(
            P("context", "tensor"),
            P("context", "tensor"),
            P("context", "tensor"),
            P("tensor", None),
            P("tensor"),
            P(("context", "tensor"), None),
            P("context", "tensor"),
        ),
        check_vma=False,
    )
```

```python
import jax
import jax.numpy as jnp
from jax import lax
from jax.experimental import pallas as pl
from jax.experimental.pallas import tpu as pltpu
from jax.sharding import PartitionSpec as P

MESH = pl.DeviceIdType.MESH
BF16 = jnp.bfloat16
F32 = jnp.float32

NZ, NYL, NCORE, NYH, NX = 8, 2, 2, 2, 4
NQ = NZ * NYL
NT = NYH * NX
TAPS = 128
ROWS = 128
CH = 512
SUB = 16
D = 8192
WIDE = D // NQ
CHUNKS = 4
CCOLS = D // CHUNKS
X_FIRST = (0,)
ORDER = (0, 1, 7, 2, 6, 3, 5, 4)
VMEM_LIMIT = 63 << 20
PIECES = (1, 1, 1, 2, 1, 1, 4)


def kernel(
    x_hbm, q_hbm, k_hbm, v_hbm, g_hbm, taps_hbm, gain_hbm, w_hbm,
    qg_hbm, kg_hbm, vg_hbm, fg_hbm, sg_hbm, ig_hbm, wg_hbm,
    qv, kv, vv, gv, taps_v, gain_v, x_v, w_v,
    inner, delta, halo_d, halo_i, tapst, dext, iext, d8, e8, back, mix,
    qgv, kgv, xa, ga, tpart, yr, sums, from_left, from_right, left_sum, right_sum, ysend, isum, ig, wacc, wrecv, wout,
    fpart, fcore, fsum, frs, ffull, fgt, sgv,
    in_sems, out_sems, halo_s, halo_r, a2a_s, a2a_r, ag_s, ag_r, b_s, b_r, c_s, c_r,
    core_s, core_r, rs_s, rs_r, fa_s, fa_r,
):
    con = lax.axis_index("context")
    ten = lax.axis_index("tensor")
    z, yl, core = con // 4, (con // 2) % 2, con % 2
    yh, x = ten // 4, ten % 4
    q = con // 2

    def at(zz, yy, cc):
        return (zz % NZ) * 4 + (yy % 2) * 2 + cc % 2

    def ten_at(hh, xx):
        return (hh % 2) * 4 + xx % 4

    def remote(src, dst, ss, rs, device):
        return pltpu.make_async_remote_copy(
            src_ref=src, dst_ref=dst, send_sem=ss, recv_sem=rs, device_id=device, device_id_type=MESH
        )

    loads = [
        pltpu.make_async_copy(src, dst, in_sems.at[i])
        for i, (src, dst) in enumerate(
            [(k_hbm, kv), (v_hbm, vv), (g_hbm, gv), (q_hbm, qv), (taps_hbm, taps_v), (gain_hbm, gain_v), (x_hbm, x_v), (w_hbm, w_v)]
        )
    ]
    for copy in loads:
        copy.start()

    barrier = pltpu.get_barrier_semaphore()
    above = (con + 1) % 32
    below = (con + 31) % 32

    def greet(device):
        pl.semaphore_signal(barrier, inc=1, device_id=device, device_id_type=MESH)

    greet((above, ten))
    greet((below, ten))
    greet((at(z, yl, core + 1), ten))

    def greet_q(i, carry):
        greet((at(z + i // 2, yl + i % 2, core), ten))
        return carry

    lax.fori_loop(1, NQ, greet_q, 0)

    def greet_t(i, carry):
        greet((con, (ten + i) % NT))
        return carry

    lax.fori_loop(1, NT, greet_t, 0)

    loads[0].wait()
    loads[1].wait()
    loads[2].wait()
    loads[3].wait()
    inner[...] = (kv[...].astype(F32) * vv[...].astype(F32)).astype(BF16)
    delta[...] = (gv[...].astype(F32) * qv[...].astype(F32)).astype(BF16)
    pl.semaphore_wait(barrier, 3 + (NQ - 1) + (NT - 1))

    halo_delta = remote(delta, halo_d, halo_s.at[0], halo_r.at[0], (below, ten))
    halo_inner = remote(inner, halo_i, halo_s.at[1], halo_r.at[1], (above, ten))
    halo_delta.start()

    own_x = pltpu.make_async_copy(
        x_v.at[:, pl.ds(pl.multiple_of(q * WIDE, WIDE), WIDE)], xa.at[0, 0], in_sems.at[8]
    )
    loads[6].wait()
    own_x.start()

    def a2a_copy(slot):
        dest = ((z + ORDER[slot // 2]) % NZ) * 2 + (yl + slot % 2) % 2
        return remote(
            x_v.at[:, pl.ds(pl.multiple_of(dest * WIDE, WIDE), WIDE)],
            xa.at[slot, 0],
            a2a_s.at[slot],
            a2a_r.at[slot],
            (dest * 2 + core, ten),
        )

    for slot in range(1, NQ):
        a2a_copy(slot).start()
    halo_inner.start()

    dext[pl.ds(0, ROWS), :] = delta[...].astype(F32)
    iext[pl.ds(ROWS, ROWS), :] = inner[...].astype(F32)

    loads[4].wait()
    loads[5].wait()
    tapst[...] = taps_v[...].astype(F32).T

    for r in range(8):
        d8[r, pl.ds(0, 15)] = dext[pl.ds(r, 120), :].reshape(15, 8, CH)

    def lanes(l):
        return pl.ds(pl.multiple_of(l * 128, 128), 128)

    def tap_row(j, cols):
        return jnp.broadcast_to(tapst[pl.ds(j, 1), cols], (8, 128))

    def chain(taps, tiles):
        total = taps[0] * tiles[0]
        for tap, tile in zip(taps[1:], tiles[1:]):
            total = total + tap * tile
        return total

    def back_own(l, carry):
        cols = lanes(l)
        gain = jnp.broadcast_to(gain_v[:, cols], (8, 128))
        for r in range(8):
            tiles = [d8[r, k, :, cols] for k in range(15)]
            taps = [tap_row(8 * a + r, cols) for a in range(15)]
            for i in range(15):
                total = chain(taps[: 15 - i], tiles[i:])
                back[i, :, cols] = total + gain * tiles[i] if r == 0 else back[i, :, cols] + total
        back[15, :, cols] = gain * dext[pl.ds(120, 8), cols]
        return carry

    def back_halo(l, carry):
        cols = lanes(l)
        for r in range(8):
            tiles = [d8[r, 15 + k, :, cols] for k in range(16)]
            taps = [tap_row(8 * a + r, cols) for a in range(16)]
            for i in range(16):
                back[i, :, cols] = back[i, :, cols] + chain(taps[15 - i :], tiles[: i + 1])
        return carry

    lax.fori_loop(0, 4, back_own, 0)

    x_up, x_down = ten_at(yh, x + 1), ten_at(yh, x + 3)
    other = ten_at(yh + 1, x)

    def ag_copy(index, phase, source, target, device):
        slots = pl.ds(8 * phase, 8)
        return remote(xa.at[slots, source], xa.at[slots, target], ag_s.at[index], ag_r.at[index], (con, device))

    def ag_y(phase):
        return ag_copy(phase, phase, 0, 1, other)

    def ag_x(phase, row, way):
        index = 2 + phase * 4 + row * 2 + way
        return ag_copy(index, phase, row, 2 + 2 * row + way, x_down if way else x_up)

    def ag_far(phase, row):
        index = 10 + phase * 2 + row
        return ag_copy(index, phase, 2 + 2 * row + phase, 6 + row, x_down if phase else x_up)

    def ag_own(phase):
        if phase == 0:
            own_x.wait()
        for slot in range(max(1, 8 * phase), 8 * phase + 8):
            a2a_copy(slot).wait_recv()
        ag_y(phase).start()
        ag_x(phase, 0, 0).start()
        ag_x(phase, 0, 1).start()

    def ag_other(phase):
        ag_y(phase).wait_recv()
        ag_x(phase, 1, 0).start()
        ag_x(phase, 1, 1).start()

    def ag_forward(phase, row):
        ag_x(phase, row, phase).wait_recv()
        ag_far(phase, row).start()

    ag_own(0)

    halo_delta.wait_recv()
    keep_d = jnp.where(con == 31, 0.0, 1.0).astype(F32)
    dext[pl.ds(ROWS, ROWS), :] = halo_d[...].astype(F32) * keep_d
    for r in range(8):
        d8[r, pl.ds(15, 16)] = dext[pl.ds(120 + r, ROWS), :].reshape(16, 8, CH)
    lax.fori_loop(0, 4, back_halo, 0)

    backs = back[...].reshape(ROWS, CH)
    ga[0] = (backs * kv[...].astype(F32)).astype(BF16)

    def b_copy(index, source, target, device):
        return remote(ga.at[source], ga.at[target], b_s.at[index], b_r.at[index], (device, ten))

    up, down = at(z + 1, yl, core), at(z + 7, yl, core)

    def slot_of(dz, rel):
        return 2 * ORDER.index(dz % NZ) + rel

    def right(d, rel):
        return b_copy(1 + (d - 1) * 4 + rel, slot_of(d - 1, rel), slot_of(d, rel), up)

    def left(d, rel):
        return b_copy(1 + (d - 1) * 4 + 2 + rel, slot_of(1 - d, rel), slot_of(-d, rel), down)

    def forward(d, rel):
        right(d, rel).wait_recv()
        if d < 3 or rel == 0:
            right(d + 1, rel).start()
        left(d, rel).wait_recv()
        if d < 3 or rel == 1:
            left(d + 1, rel).start()

    right(1, 0).start()
    left(1, 0).start()
    across = b_copy(0, 0, 1, at(z, yl + 1, core))
    across.start()

    ag_own(1)

    loads[7].wait()

    ccols = [pl.ds(chunk * CCOLS, CCOLS) for chunk in range(CHUNKS)]
    first_half = [pl.ds(chunk * CCOLS, CCOLS // 2) for chunk in range(CHUNKS)]
    second_half = [pl.ds(chunk * CCOLS + CCOLS // 2, CCOLS // 2) for chunk in range(CHUNKS)]
    lo, hi = pl.ds(0, CCOLS // 2), pl.ds(CCOLS // 2, CCOLS // 2)
    hops = [(x + dx) % 4 for dx in range(4)]

    def c_remote(chunk, kind, src, dst, device):
        index = chunk * 8 + kind
        return remote(src, dst, c_s.at[index], c_r.at[index], (con, device))

    def y_copy(chunk):
        return c_remote(chunk, 0, tpart.at[1 - yh, :, :, ccols[chunk]], yr.at[:, :, ccols[chunk]], other)

    def x_refs(chunk, dx, part):
        if chunk in X_FIRST:
            return tpart.at[:, hops[dx], :, part[chunk]]
        return sums.at[pl.ds(0, 1), dx, :, part[chunk]]

    def groups(chunk):
        return pl.ds(0, 2) if chunk in X_FIRST else pl.ds(0, 1)

    def x_copy(chunk, kind):
        g = groups(chunk)
        src, dst, device = (
            (x_refs(chunk, 2, first_half), from_left.at[chunk, g, :, lo], x_up),
            (x_refs(chunk, 2, second_half), from_right.at[chunk, g, :, hi], x_down),
            (x_refs(chunk, 1, second_half), left_sum.at[chunk, g, :, hi], x_up),
            (x_refs(chunk, 3, first_half), right_sum.at[chunk, g, :, lo], x_down),
            (sums.at[g, 1, :, first_half[chunk]], left_sum.at[chunk, g, :, lo], x_up),
            (sums.at[g, 3, :, second_half[chunk]], right_sum.at[chunk, g, :, hi], x_down),
        )[kind]
        return c_remote(chunk, 1 + kind, src, dst, device)

    def yx_copy(chunk):
        return c_remote(chunk, 7, ysend.at[:, ccols[chunk]], yr.at[0, :, ccols[chunk]], other)

    def f32(ref, *index):
        return ref[index].astype(F32)

    def terms(chunk):
        def part(n, carry):
            cols = pl.ds(pl.multiple_of(chunk * CCOLS + n * 512, 512), 512)
            product = lax.dot_general(ga[0], w_v[cols, :], (((1,), (1,)), ((), ())), preferred_element_type=F32)
            tpart[:, :, :, cols] = product.astype(BF16).reshape(NYH, NX, SUB, 512)
            return carry

        lax.fori_loop(0, CCOLS // 512, part, 0)
        if chunk in X_FIRST:
            for kind in range(4):
                x_copy(chunk, kind).start()
        else:
            y_copy(chunk).start()

    def c_sum_y(chunk):
        y_copy(chunk).wait_recv()
        for dx in (2, 1, 3):
            total = f32(tpart, yh, hops[dx], slice(None), ccols[chunk]) + f32(yr, hops[dx], slice(None), ccols[chunk])
            sums[0, dx, :, ccols[chunk]] = total.astype(BF16)
        for kind in range(4):
            x_copy(chunk, kind).start()

    def c_pass_on(chunk):
        g = groups(chunk)
        for kind, dx, part, here, arrived in ((0, 1, first_half, lo, from_left), (1, 3, second_half, hi, from_right)):
            x_copy(chunk, kind).wait_recv()
            mine = x_refs(chunk, dx, part)[...].astype(F32)
            sums[g, dx, :, part[chunk]] = (mine + f32(arrived, chunk, g, slice(None), here)).astype(BF16)
            x_copy(chunk, kind + 4).start()

    def c_wait_x(chunk):
        for kind in range(2, 6):
            x_copy(chunk, kind).wait_recv()

    def c_turn_y(chunk):
        c_wait_x(chunk)
        cols = ccols[chunk]

        def total(h):
            return f32(tpart, h, x, slice(None), cols) + f32(left_sum, chunk, h) + f32(right_sum, chunk, h)

        ysend[:, cols] = total(1 - yh).astype(BF16)
        yx_copy(chunk).start()
        isum[:, cols] = total(yh)

    def c_end(chunk):
        cols = ccols[chunk]
        if chunk in X_FIRST:
            yx_copy(chunk).wait_recv()
            ig[:, cols] = (isum[:, cols] + f32(yr, 0, slice(None), cols)).astype(BF16)
        else:
            c_wait_x(chunk)
            total = f32(tpart, yh, x, slice(None), cols) + f32(yr, x, slice(None), cols)
            ig[:, cols] = (total + f32(left_sum, chunk, 0) + f32(right_sum, chunk, 0)).astype(BF16)

    def c_sent(chunk):
        for kind in range(6):
            x_copy(chunk, kind).wait_send()
        (yx_copy if chunk in X_FIRST else y_copy)(chunk).wait_send()

    def filter_tile(l, carry):
        cols = lanes(l)
        rows = [iext[pl.ds(ROWS + 8 * i, 8), cols] for i in range(16)]
        for r in range(8):
            tiles = [d8[r, k, :, cols] for k in range(31)]
            for a in range(16):
                total = rows[0] * tiles[a]
                for i in range(1, 16):
                    total = total + rows[i] * tiles[i + a]
                fpart[pl.ds(8 * a + r, 1), cols] = jnp.sum(total, axis=0, keepdims=True)
        return carry

    terms(0)
    ag_other(0)
    terms(1)
    forward(1, 0)
    across.wait_recv()
    right(1, 1).start()
    left(1, 1).start()
    ag_forward(0, 0)
    lax.fori_loop(0, 4, filter_tile, 0)

    half = CH // 2
    mine = pl.ds(pl.multiple_of(core * half, half), half)
    theirs = pl.ds(pl.multiple_of((1 - core) * half, half), half)
    partner = (at(z, yl, core + 1), ten)
    f_core = remote(fpart.at[:, theirs], fcore, core_s.at[0], core_r.at[0], partner)
    f_core.start()
    ag_other(1)
    forward(2, 0)
    terms(2)
    c_pass_on(0)
    ag_forward(1, 0)
    ag_forward(0, 1)
    forward(1, 1)
    terms(3)

    f_core.wait_recv()
    fsum[...] = fpart[:, mine] + fcore[...]

    def q_of(i, way):
        return ((z + NZ + way * (i // 2)) % NZ) * 2 + (yl + i % 2) % 2

    def rs_copy(i):
        dest = q_of(i, 1)
        return remote(
            fsum.at[pl.ds(pl.multiple_of(dest * 8, 8), 8), :], frs.at[i], rs_s.at[i], rs_r.at[i], (dest * 2 + core, ten)
        )

    def rs_start(i, carry):
        rs_copy(i).start()
        return carry

    lax.fori_loop(1, NQ, rs_start, 0)

    kgv[...] = (back[...].reshape(ROWS, CH) * vv[...].astype(F32)).astype(BF16)
    out_copies = [
        pltpu.make_async_copy(kgv, kg_hbm, out_sems.at[0]),
        pltpu.make_async_copy(ga.at[0], vg_hbm, out_sems.at[1]),
    ]
    for copy in out_copies:
        copy.start()


    halo_inner.wait_recv()
    keep_i = jnp.where(con == 0, 0.0, 1.0).astype(F32)
    iext[pl.ds(0, ROWS), :] = halo_i[...].astype(F32) * keep_i
    e8[0] = iext[...].reshape(32, 8, CH)
    for r in range(1, 8):
        e8[r, pl.ds(0, 31)] = iext[pl.ds(r, 248), :].reshape(31, 8, CH)

    def mixed_tile(l, carry):
        cols = lanes(l)
        gain = jnp.broadcast_to(gain_v[:, cols], (8, 128))
        for r in range(8):
            skip = 1 if r == 0 else 0
            taps = [tap_row(TAPS - 8 * (b + skip) - r, cols) for b in range(16)]
            for start in (0, 8):
                tiles = [e8[r, start + k + skip, :, cols] for k in range(23)]
                for i in range(8):
                    total = chain(taps, tiles[i : i + 16])
                    at_i = (start + i, slice(None), cols)
                    mix[at_i] = total + gain * tiles[i + 15] if r == 0 else mix[at_i] + total
        mixed = mix[:, :, cols].reshape(ROWS, 128)
        qgv[:, cols] = (gv[:, cols].astype(F32) * mixed).astype(BF16)
        return carry

    c_sum_y(1)
    forward(3, 0)
    lax.fori_loop(0, 2, mixed_tile, 0)
    ag_forward(1, 1)
    forward(2, 1)
    lax.fori_loop(2, 4, mixed_tile, 0)
    copy = pltpu.make_async_copy(qgv, qg_hbm, out_sems.at[2])
    copy.start()
    out_copies.append(copy)

    far, other_far = ten_at(yh, x + 2), ten_at(yh + 1, x + 2)
    sources = (ten, other, x_down, x_up, ten_at(yh + 1, x + 3), ten_at(yh + 1, x + 1), far, other_far)

    def product(phase, pair, m):
        slots = pl.ds(8 * phase, 8)
        cols = pl.ds(pl.multiple_of(m * 256, 256), 256)
        lhs = xa[slots, pl.ds(2 * pair, 2), :, cols].reshape(256, 256)

        def token_rows(part):
            return ga[slots, pl.ds(pl.multiple_of(part * SUB, SUB), SUB), :]

        rhs = jnp.stack([token_rows(sources[2 * pair]), token_rows(sources[2 * pair + 1])], axis=1).reshape(256, CH)
        new = lax.dot_general(lhs, rhs, (((0,), (0,)), ((), ())), preferred_element_type=F32)
        if phase == 0 and pair == 0:
            wacc[cols, :] = new
        else:
            wacc[cols, :] += new

    if 0 in X_FIRST:
        c_turn_y(0)
    c_pass_on(1)
    c_sum_y(2)
    forward(3, 1)

    def rs_wait(i, carry):
        rs_copy(i).wait_recv()
        return carry

    lax.fori_loop(1, NQ, rs_wait, 0)
    total = fsum[pl.ds(pl.multiple_of(q * 8, 8), 8), :]
    for i in range(1, NQ):
        total = total + frs[i]
    my_rows = pl.ds(pl.multiple_of(q * 8, 8), 8)
    ffull[my_rows, mine] = total

    def fa_copy(i, source):
        ref = ffull.at[pl.ds(pl.multiple_of(source * 8, 8), 8), mine]
        return remote(ref, ref, fa_s.at[i], fa_r.at[i], (q_of(i, 1) * 2 + core, ten))

    def fa_start(i, carry):
        fa_copy(i, q).start()
        return carry

    lax.fori_loop(1, NQ, fa_start, 0)

    product(0, 0, 0)
    product(0, 0, 1)
    ag_x(0, 0, 1).wait_recv()
    product(0, 1, 0)
    product(0, 1, 1)
    ag_x(0, 1, 1).wait_recv()
    product(0, 2, 0)
    product(0, 2, 1)
    c_pass_on(2)
    c_sum_y(3)
    right(4, 0).wait_recv()
    left(4, 1).wait_recv()
    ag_far(0, 0).wait_recv()
    ag_far(0, 1).wait_recv()
    product(0, 3, 0)
    product(0, 3, 1)
    c_end(0)
    c_end(1)
    c_end(2)
    c_pass_on(3)

    def fa_wait(i, carry):
        fa_copy(i, q_of(i, -1)).wait_recv()
        return carry

    lax.fori_loop(1, NQ, fa_wait, 0)
    f_back = remote(ffull.at[:, mine], ffull.at[:, mine], core_s.at[1], core_r.at[1], partner)
    f_back.start()
    product(1, 0, 0)
    product(1, 0, 1)
    ag_x(1, 0, 0).wait_recv()
    product(1, 1, 0)
    product(1, 1, 1)
    ag_x(1, 1, 0).wait_recv()
    product(1, 2, 0)
    product(1, 2, 1)
    ag_far(1, 0).wait_recv()
    ag_far(1, 1).wait_recv()
    partner_rows = pl.ds(pl.multiple_of((1 - core) * 256, 256), 256)
    product(1, 3, 1 - core)
    w_core = remote(wacc.at[partner_rows, :], wrecv, core_s.at[2], core_r.at[2], partner)
    w_core.start()
    product(1, 3, core)

    f_back_wait = remote(ffull.at[:, theirs], ffull.at[:, theirs], core_s.at[1], core_r.at[1], partner)
    f_back_wait.wait_recv()
    fgt[...] = ffull[...].T
    sgv[...] = ffull[pl.ds(0, 1), :]
    for copy in (
        pltpu.make_async_copy(fgt, fg_hbm, out_sems.at[3]),
        pltpu.make_async_copy(sgv, sg_hbm, out_sems.at[4]),
    ):
        copy.start()
        out_copies.append(copy)

    c_end(3)
    copy = pltpu.make_async_copy(ig, ig_hbm, out_sems.at[5])
    copy.start()
    out_copies.append(copy)

    w_core.wait_recv()
    for n in range(4):
        rows = pl.ds(64 * n, 64)
        wout[rows, :] = wacc[pl.ds(pl.multiple_of(core * 256 + 64 * n, 64), 64), :] + wrecv[rows, :]
        copy = pltpu.make_async_copy(wout.at[rows, :], wg_hbm.at[rows, :], out_sems.at[6 + n])
        copy.start()
        out_copies.append(copy)

    halo_delta.wait_send()
    halo_inner.wait_send()

    def sent(i, carry):
        rs_copy(i).wait_send()
        fa_copy(i, q).wait_send()
        return carry

    lax.fori_loop(1, NQ, sent, 0)
    for slot in range(1, NQ):
        a2a_copy(slot).wait_send()
    for phase in range(2):
        ag_y(phase).wait_send()
        for row in range(2):
            ag_x(phase, row, 0).wait_send()
            ag_x(phase, row, 1).wait_send()
            ag_far(phase, row).wait_send()
    across.wait_send()
    for rel in range(2):
        for d in range(1, 4):
            right(d, rel).wait_send()
            left(d, rel).wait_send()
    right(4, 0).wait_send()
    left(4, 1).wait_send()
    for chunk in range(CHUNKS):
        c_sent(chunk)
    f_core.wait_send()
    f_back.wait_send()
    w_core.wait_send()
    for copy in out_copies:
        copy.wait()


def finish(*refs):
    ins, outs, held, (in_sems, out_sems) = refs[:7], refs[7:14], refs[14:21], refs[21:]
    reads, writes = [], []
    for i, pieces in enumerate(PIECES):
        rows = ins[i].shape[0] // pieces
        for n in range(pieces):
            part = pl.ds(rows * n, rows)
            at = len(reads)
            reads.append(pltpu.make_async_copy(ins[i].at[part, :], held[i].at[part, :], in_sems.at[at]))
            writes.append(pltpu.make_async_copy(held[i].at[part, :], outs[i].at[part, :], out_sems.at[at]))
    for read in reads:
        read.start()
    for read, write in zip(reads, writes):
        read.wait()
        write.start()
    for write in writes:
        write.wait()


def local(layer_input, query_stream, key_stream, value_stream, output_grad, filter_taps, skip_gain, value_weight):
    shape = jax.ShapeDtypeStruct
    vm = pltpu.VMEM
    dma = pltpu.SemaphoreType.DMA
    outs = pl.pallas_call(
        kernel,
        out_shape=(
            shape((ROWS, CH), BF16),
            shape((ROWS, CH), BF16),
            shape((ROWS, CH), BF16),
            shape((CH, TAPS), F32),
            shape((1, CH), F32),
            shape((SUB, D), BF16),
            shape((256, CH), F32),
        ),
        in_specs=[pl.BlockSpec(memory_space=pl.ANY)] * 8,
        out_specs=[pl.BlockSpec(memory_space=pl.ANY)] * 7,
        scratch_shapes=[
            vm((ROWS, CH), BF16),
            vm((ROWS, CH), BF16),
            vm((ROWS, CH), BF16),
            vm((ROWS, CH), BF16),
            vm((CH, TAPS), BF16),
            vm((1, CH), F32),
            vm((SUB, D), BF16),
            vm((D, CH), BF16),
            vm((ROWS, CH), BF16),
            vm((ROWS, CH), BF16),
            vm((ROWS, CH), BF16),
            vm((ROWS, CH), BF16),
            vm((TAPS, CH), F32),
            vm((2 * ROWS, CH), F32),
            vm((2 * ROWS, CH), F32),
            vm((8, 32, 8, CH), F32),
            vm((8, 32, 8, CH), F32),
            vm((16, 8, CH), F32),
            vm((16, 8, CH), F32),
            vm((ROWS, CH), BF16),
            vm((ROWS, CH), BF16),
            vm((NQ, NT, SUB, WIDE), BF16),
            vm((NQ, ROWS, CH), BF16),
            vm((NYH, NX, SUB, D), BF16),
            vm((NX, SUB, D), BF16),
            vm((NYH, NX, SUB, D), BF16),
            vm((CHUNKS, NYH, SUB, CCOLS), BF16),
            vm((CHUNKS, NYH, SUB, CCOLS), BF16),
            vm((CHUNKS, NYH, SUB, CCOLS), BF16),
            vm((CHUNKS, NYH, SUB, CCOLS), BF16),
            vm((SUB, D), BF16),
            vm((SUB, D), F32),
            vm((SUB, D), BF16),
            vm((WIDE, CH), F32),
            vm((256, CH), F32),
            vm((256, CH), F32),
            vm((TAPS, CH), F32),
            vm((TAPS, CH // 2), F32),
            vm((TAPS, CH // 2), F32),
            vm((NQ, 8, CH // 2), F32),
            vm((TAPS, CH), F32),
            vm((CH, TAPS), F32),
            vm((1, CH), F32),
            dma((9,)),
            dma((10,)),
            dma((2,)), dma((2,)),
            dma((NQ,)), dma((NQ,)),
            dma((14,)), dma((14,)),
            dma((17,)), dma((17,)),
            dma((8 * CHUNKS,)), dma((8 * CHUNKS,)),
            dma((3,)), dma((3,)),
            dma((NQ,)), dma((NQ,)),
            dma((NQ,)), dma((NQ,)),
        ],
        compiler_params=pltpu.CompilerParams(
            collective_id=0, has_side_effects=True, vmem_limit_bytes=VMEM_LIMIT
        ),
        name="hyena_back",
    )(
        layer_input, query_stream, key_stream, value_stream, output_grad, filter_taps,
        skip_gain.reshape(1, CH), value_weight,
    )
    outs = pl.pallas_call(
        finish,
        out_shape=tuple(shape(out.shape, out.dtype) for out in outs),
        in_specs=[pl.BlockSpec(memory_space=pl.ANY)] * 7,
        out_specs=[pl.BlockSpec(memory_space=pl.ANY)] * 7,
        scratch_shapes=[vm(out.shape, out.dtype) for out in outs] + [dma((sum(PIECES),)), dma((sum(PIECES),))],
        compiler_params=pltpu.CompilerParams(vmem_limit_bytes=VMEM_LIMIT),
        name="finish",
    )(*outs)
    query_grad, key_grad, value_grad, filter_grad, skip_grad, input_grad, weight_grad = outs
    return (query_grad, key_grad, value_grad, filter_grad, skip_grad.reshape(CH), input_grad, weight_grad)


def solution(mesh):
    placed = (
        P(("context", "tensor"), None),
        P("context", "tensor"),
        P("context", "tensor"),
        P("context", "tensor"),
        P("context", "tensor"),
        P("tensor", None),
        P("tensor"),
        P(None, "tensor"),
    )
    return jax.shard_map(
        local,
        mesh=mesh,
        in_specs=placed,
        out_specs=(
            P("context", "tensor"),
            P("context", "tensor"),
            P("context", "tensor"),
            P("tensor", None),
            P("tensor"),
            P(("context", "tensor"), None),
            P("context", "tensor"),
        ),
        check_vma=False,
    )
```

```python
import jax
import jax.numpy as jnp
from jax import lax
from jax.experimental import pallas as pl
from jax.experimental.pallas import tpu as pltpu
from jax.sharding import PartitionSpec as P

MESH = pl.DeviceIdType.MESH
BF16 = jnp.bfloat16
F32 = jnp.float32

NZ, NYL, NCORE, NYH, NX = 8, 2, 2, 2, 4
NQ = NZ * NYL
NT = NYH * NX
TAPS = 128
ROWS = 128
CH = 512
SUB = 16
D = 8192
WIDE = D // NQ
CHUNKS = 4
CCOLS = D // CHUNKS
X_FIRST = (0,)
ORDER = (0, 1, 7, 2, 6, 3, 5, 4)
VMEM_LIMIT = 63 << 20
PIECES = (1, 1, 1, 2, 1, 1, 4)


def kernel(
    x_hbm, q_hbm, k_hbm, v_hbm, g_hbm, taps_hbm, gain_hbm, w_hbm,
    qg_hbm, kg_hbm, vg_hbm, fg_hbm, sg_hbm, ig_hbm, wg_hbm,
    qv, kv, vv, gv, taps_v, gain_v, x_v, w_v,
    inner, delta, halo_d, halo_i, tapst, dext, iext, d8, e8, back, mix,
    qgv, kgv, xa, ga, tpart, yr, sums, from_left, from_right, left_sum, right_sum, ysend, isum, ig, wacc, wrecv, wout,
    fpart, fcore, fsum, frs, ffull, fgt, sgv,
    in_sems, out_sems, halo_s, halo_r, a2a_s, a2a_r, ag_s, ag_r, b_s, b_r, c_s, c_r,
    core_s, core_r, rs_s, rs_r, fa_s, fa_r,
):
    con = lax.axis_index("context")
    ten = lax.axis_index("tensor")
    z, yl, core = con // 4, (con // 2) % 2, con % 2
    yh, x = ten // 4, ten % 4
    q = con // 2

    def at(zz, yy, cc):
        return (zz % NZ) * 4 + (yy % 2) * 2 + cc % 2

    def ten_at(hh, xx):
        return (hh % 2) * 4 + xx % 4

    def remote(src, dst, ss, rs, device):
        return pltpu.make_async_remote_copy(
            src_ref=src, dst_ref=dst, send_sem=ss, recv_sem=rs, device_id=device, device_id_type=MESH
        )

    loads = [
        pltpu.make_async_copy(src, dst, in_sems.at[i])
        for i, (src, dst) in enumerate(
            [(k_hbm, kv), (v_hbm, vv), (g_hbm, gv), (q_hbm, qv), (taps_hbm, taps_v), (gain_hbm, gain_v), (x_hbm, x_v), (w_hbm, w_v)]
        )
    ]
    barrier = pltpu.get_barrier_semaphore()
    above = (con + 1) % 32
    below = (con + 31) % 32

    def greet(device):
        pl.semaphore_signal(barrier, inc=1, device_id=device, device_id_type=MESH)

    for dz in (4, 3, 5, 2, 6, 1, 7, 0):
        for dy in range(2):
            if (dz, dy) != (0, 0):
                greet((at(z + dz, yl + dy, core), ten))
    for i in (6, 2, 5, 7, 4, 1, 3):
        greet((con, (ten + i) % NT))
    greet((above, ten))
    greet((below, ten))
    greet((at(z, yl, core + 1), ten))
    for copy in loads:
        copy.start()


    loads[0].wait()
    loads[1].wait()
    loads[2].wait()
    loads[3].wait()
    inner[...] = (kv[...].astype(F32) * vv[...].astype(F32)).astype(BF16)
    delta[...] = (gv[...].astype(F32) * qv[...].astype(F32)).astype(BF16)
    pl.semaphore_wait(barrier, 3 + (NQ - 1) + (NT - 1))

    halo_delta = remote(delta, halo_d, halo_s.at[0], halo_r.at[0], (below, ten))
    halo_inner = remote(inner, halo_i, halo_s.at[1], halo_r.at[1], (above, ten))
    halo_delta.start()

    own_x = pltpu.make_async_copy(
        x_v.at[:, pl.ds(pl.multiple_of(q * WIDE, WIDE), WIDE)], xa.at[0, 0], in_sems.at[8]
    )
    loads[6].wait()
    own_x.start()

    def a2a_copy(slot):
        dest = ((z + ORDER[slot // 2]) % NZ) * 2 + (yl + slot % 2) % 2
        return remote(
            x_v.at[:, pl.ds(pl.multiple_of(dest * WIDE, WIDE), WIDE)],
            xa.at[slot, 0],
            a2a_s.at[0],
            a2a_r.at[slot // 8],
            (dest * 2 + core, ten),
        )

    for slot in range(1, NQ):
        a2a_copy(slot).start()
    halo_inner.start()

    dext[pl.ds(0, ROWS), :] = delta[...].astype(F32)
    iext[pl.ds(ROWS, ROWS), :] = inner[...].astype(F32)

    loads[4].wait()
    loads[5].wait()
    tapst[...] = taps_v[...].astype(F32).T

    for r in range(8):
        d8[r, pl.ds(0, 15)] = dext[pl.ds(r, 120), :].reshape(15, 8, CH)

    def lanes(l):
        return pl.ds(pl.multiple_of(l * 128, 128), 128)

    def tap_row(j, cols):
        return jnp.broadcast_to(tapst[pl.ds(j, 1), cols], (8, 128))

    def chain(taps, tiles):
        total = taps[0] * tiles[0]
        for tap, tile in zip(taps[1:], tiles[1:]):
            total = total + tap * tile
        return total

    def back_own(l, carry):
        cols = lanes(l)
        gain = jnp.broadcast_to(gain_v[:, cols], (8, 128))
        for r in range(8):
            tiles = [d8[r, k, :, cols] for k in range(15)]
            taps = [tap_row(8 * a + r, cols) for a in range(15)]
            for i in range(15):
                total = chain(taps[: 15 - i], tiles[i:])
                back[i, :, cols] = total + gain * tiles[i] if r == 0 else back[i, :, cols] + total
        back[15, :, cols] = gain * dext[pl.ds(120, 8), cols]
        return carry

    def back_halo(l, carry):
        cols = lanes(l)
        for r in range(8):
            tiles = [d8[r, 15 + k, :, cols] for k in range(16)]
            taps = [tap_row(8 * a + r, cols) for a in range(16)]
            for i in range(16):
                back[i, :, cols] = back[i, :, cols] + chain(taps[15 - i :], tiles[: i + 1])
        return carry

    lax.fori_loop(0, 4, back_own, 0)

    x_up, x_down = ten_at(yh, x + 1), ten_at(yh, x + 3)
    other = ten_at(yh + 1, x)

    def ag_copy(index, phase, source, target, device):
        slots = pl.ds(8 * phase, 8)
        return remote(xa.at[slots, source], xa.at[slots, target], ag_s.at[0], ag_r.at[index], (con, device))

    def ag_y(phase):
        return ag_copy(phase, phase, 0, 1, other)

    def ag_x(phase, row, way):
        index = 2 + phase * 4 + row * 2 + way
        return ag_copy(index, phase, row, 2 + 2 * row + way, x_down if way else x_up)

    def ag_far(phase, row):
        index = 10 + phase * 2 + row
        return ag_copy(index, phase, 2 + 2 * row + phase, 6 + row, x_down if phase else x_up)

    def ag_own(phase):
        if phase == 0:
            own_x.wait()
        group = xa.at[pl.ds(8, 8), 0] if phase else xa.at[pl.ds(1, 7), 0]
        remote(group, group, a2a_s.at[0], a2a_r.at[phase], (above, ten)).wait_recv()
        ag_y(phase).start()
        ag_x(phase, 0, 0).start()
        ag_x(phase, 0, 1).start()

    def ag_other(phase):
        ag_y(phase).wait_recv()
        ag_x(phase, 1, 0).start()
        ag_x(phase, 1, 1).start()

    def ag_forward(phase, row):
        ag_x(phase, row, phase).wait_recv()
        ag_far(phase, row).start()


    halo_delta.wait_recv()
    keep_d = jnp.where(con == 31, 0.0, 1.0).astype(F32)
    dext[pl.ds(ROWS, ROWS), :] = halo_d[...].astype(F32) * keep_d
    for r in range(8):
        d8[r, pl.ds(15, 16)] = dext[pl.ds(120 + r, ROWS), :].reshape(16, 8, CH)
    lax.fori_loop(0, 4, back_halo, 0)

    backs = back[...].reshape(ROWS, CH)
    ga[0] = (backs * kv[...].astype(F32)).astype(BF16)

    def b_copy(index, source, target, device):
        return remote(ga.at[source], ga.at[target], b_s.at[0], b_r.at[index], (device, ten))

    up, down = at(z + 1, yl, core), at(z + 7, yl, core)

    def slot_of(dz, rel):
        return 2 * ORDER.index(dz % NZ) + rel

    def right(d, rel):
        return b_copy(1 + (d - 1) * 4 + rel, slot_of(d - 1, rel), slot_of(d, rel), up)

    def left(d, rel):
        return b_copy(1 + (d - 1) * 4 + 2 + rel, slot_of(1 - d, rel), slot_of(-d, rel), down)

    def forward(d, rel):
        right(d, rel).wait_recv()
        if d < 3 or rel == 0:
            right(d + 1, rel).start()
        left(d, rel).wait_recv()
        if d < 3 or rel == 1:
            left(d + 1, rel).start()

    right(1, 0).start()
    left(1, 0).start()
    across = b_copy(0, 0, 1, at(z, yl + 1, core))
    across.start()


    loads[7].wait()

    ccols = [pl.ds(chunk * CCOLS, CCOLS) for chunk in range(CHUNKS)]
    first_half = [pl.ds(chunk * CCOLS, CCOLS // 2) for chunk in range(CHUNKS)]
    second_half = [pl.ds(chunk * CCOLS + CCOLS // 2, CCOLS // 2) for chunk in range(CHUNKS)]
    lo, hi = pl.ds(0, CCOLS // 2), pl.ds(CCOLS // 2, CCOLS // 2)
    hops = [(x + dx) % 4 for dx in range(4)]

    def c_remote(chunk, kind, src, dst, device):
        index = chunk * 8 + kind
        return remote(src, dst, c_s.at[0], c_r.at[index], (con, device))

    def y_copy(chunk):
        return c_remote(chunk, 0, tpart.at[1 - yh, :, :, ccols[chunk]], yr.at[:, :, ccols[chunk]], other)

    def x_refs(chunk, dx, part):
        if chunk in X_FIRST:
            return tpart.at[:, hops[dx], :, part[chunk]]
        return sums.at[pl.ds(0, 1), dx, :, part[chunk]]

    def groups(chunk):
        return pl.ds(0, 2) if chunk in X_FIRST else pl.ds(0, 1)

    def x_copy(chunk, kind):
        g = groups(chunk)
        src, dst, device = (
            (x_refs(chunk, 2, first_half), from_left.at[chunk, g, :, lo], x_up),
            (x_refs(chunk, 2, second_half), from_right.at[chunk, g, :, hi], x_down),
            (x_refs(chunk, 1, second_half), left_sum.at[chunk, g, :, hi], x_up),
            (x_refs(chunk, 3, first_half), right_sum.at[chunk, g, :, lo], x_down),
            (sums.at[g, 1, :, first_half[chunk]], left_sum.at[chunk, g, :, lo], x_up),
            (sums.at[g, 3, :, second_half[chunk]], right_sum.at[chunk, g, :, hi], x_down),
        )[kind]
        return c_remote(chunk, 1 + kind, src, dst, device)

    def yx_copy(chunk):
        return c_remote(chunk, 7, ysend.at[:, ccols[chunk]], yr.at[0, :, ccols[chunk]], other)

    def f32(ref, *index):
        return ref[index].astype(F32)

    def terms(chunk):
        def part(n, carry):
            cols = pl.ds(pl.multiple_of(chunk * CCOLS + n * 512, 512), 512)
            product = lax.dot_general(ga[0], w_v[cols, :], (((1,), (1,)), ((), ())), preferred_element_type=F32)
            tpart[:, :, :, cols] = product.astype(BF16).reshape(NYH, NX, SUB, 512)
            return carry

        lax.fori_loop(0, CCOLS // 512, part, 0)
        if chunk in X_FIRST:
            for kind in range(4):
                x_copy(chunk, kind).start()
        else:
            y_copy(chunk).start()

    def c_sum_y(chunk):
        y_copy(chunk).wait_recv()
        for dx in (2, 1, 3):
            total = f32(tpart, yh, hops[dx], slice(None), ccols[chunk]) + f32(yr, hops[dx], slice(None), ccols[chunk])
            sums[0, dx, :, ccols[chunk]] = total.astype(BF16)
        for kind in range(4):
            x_copy(chunk, kind).start()

    def c_pass_on(chunk):
        g = groups(chunk)
        for kind, dx, part, here, arrived in ((0, 1, first_half, lo, from_left), (1, 3, second_half, hi, from_right)):
            x_copy(chunk, kind).wait_recv()
            mine = x_refs(chunk, dx, part)[...].astype(F32)
            sums[g, dx, :, part[chunk]] = (mine + f32(arrived, chunk, g, slice(None), here)).astype(BF16)
            x_copy(chunk, kind + 4).start()

    def c_wait_x(chunk):
        for kind in range(2, 6):
            x_copy(chunk, kind).wait_recv()

    def c_turn_y(chunk):
        c_wait_x(chunk)
        cols = ccols[chunk]

        def total(h):
            return f32(tpart, h, x, slice(None), cols) + f32(left_sum, chunk, h) + f32(right_sum, chunk, h)

        ysend[:, cols] = total(1 - yh).astype(BF16)
        yx_copy(chunk).start()
        isum[:, cols] = total(yh)

    def c_end(chunk):
        cols = ccols[chunk]
        if chunk in X_FIRST:
            yx_copy(chunk).wait_recv()
            ig[:, cols] = (isum[:, cols] + f32(yr, 0, slice(None), cols)).astype(BF16)
        else:
            c_wait_x(chunk)
            total = f32(tpart, yh, x, slice(None), cols) + f32(yr, x, slice(None), cols)
            ig[:, cols] = (total + f32(left_sum, chunk, 0) + f32(right_sum, chunk, 0)).astype(BF16)

    def filter_tile(l, carry):
        cols = lanes(l)
        rows = [iext[pl.ds(ROWS + 8 * i, 8), cols] for i in range(16)]
        for r in range(8):
            tiles = [d8[r, k, :, cols] for k in range(31)]
            for a in range(16):
                total = rows[0] * tiles[a]
                for i in range(1, 16):
                    total = total + rows[i] * tiles[i + a]
                fpart[pl.ds(8 * a + r, 1), cols] = jnp.sum(total, axis=0, keepdims=True)
        return carry

    ag_own(0)
    terms(0)
    ag_own(1)
    forward(1, 0)
    across.wait_recv()
    right(1, 1).start()
    left(1, 1).start()
    terms(1)
    lax.fori_loop(0, 2, filter_tile, 0)
    ag_other(0)
    forward(2, 0)
    ag_forward(0, 0)
    lax.fori_loop(2, 4, filter_tile, 0)

    half = CH // 2
    mine = pl.ds(pl.multiple_of(core * half, half), half)
    theirs = pl.ds(pl.multiple_of((1 - core) * half, half), half)
    partner = (at(z, yl, core + 1), ten)
    f_core = remote(fpart.at[:, theirs], fcore, core_s.at[0], core_r.at[0], partner)
    f_core.start()
    forward(1, 1)
    ag_other(1)
    terms(2)

    f_core.wait_recv()
    fsum[...] = fpart[:, mine] + fcore[...]

    def q_of(i, way):
        return ((z + NZ + way * (i // 2)) % NZ) * 2 + (yl + i % 2) % 2

    def rs_copy(i):
        dest = q_of(i, 1)
        return remote(
            fsum.at[pl.ds(pl.multiple_of(dest * 8, 8), 8), :], frs.at[i], rs_s.at[0], rs_r.at[0], (dest * 2 + core, ten)
        )

    def rs_start(i, carry):
        rs_copy(i).start()
        return carry

    lax.fori_loop(1, NQ, rs_start, 0)
    forward(3, 0)
    c_pass_on(0)
    ag_forward(1, 0)
    ag_forward(0, 1)
    terms(3)
    forward(2, 1)

    kgv[...] = (back[...].reshape(ROWS, CH) * vv[...].astype(F32)).astype(BF16)
    out_copies = [
        pltpu.make_async_copy(kgv, kg_hbm, out_sems.at[0]),
        pltpu.make_async_copy(ga.at[0], vg_hbm, out_sems.at[1]),
    ]
    for copy in out_copies:
        copy.start()


    halo_inner.wait_recv()
    keep_i = jnp.where(con == 0, 0.0, 1.0).astype(F32)
    iext[pl.ds(0, ROWS), :] = halo_i[...].astype(F32) * keep_i
    e8[0] = iext[...].reshape(32, 8, CH)
    for r in range(1, 8):
        e8[r, pl.ds(0, 31)] = iext[pl.ds(r, 248), :].reshape(31, 8, CH)

    def mixed_tile(l, carry):
        cols = lanes(l)
        gain = jnp.broadcast_to(gain_v[:, cols], (8, 128))
        for r in range(8):
            skip = 1 if r == 0 else 0
            taps = [tap_row(TAPS - 8 * (b + skip) - r, cols) for b in range(16)]
            for start in (0, 8):
                tiles = [e8[r, start + k + skip, :, cols] for k in range(23)]
                for i in range(8):
                    total = chain(taps, tiles[i : i + 16])
                    at_i = (start + i, slice(None), cols)
                    mix[at_i] = total + gain * tiles[i + 15] if r == 0 else mix[at_i] + total
        mixed = mix[:, :, cols].reshape(ROWS, 128)
        qgv[:, cols] = (gv[:, cols].astype(F32) * mixed).astype(BF16)
        return carry

    c_sum_y(1)
    lax.fori_loop(0, 2, mixed_tile, 0)
    ag_forward(1, 1)
    c_pass_on(1)
    lax.fori_loop(2, 4, mixed_tile, 0)
    copy = pltpu.make_async_copy(qgv, qg_hbm, out_sems.at[2])
    copy.start()
    out_copies.append(copy)

    forward(3, 1)
    if 0 in X_FIRST:
        c_turn_y(0)
    c_sum_y(2)

    far, other_far = ten_at(yh, x + 2), ten_at(yh + 1, x + 2)
    sources = (ten, other, x_down, x_up, ten_at(yh + 1, x + 3), ten_at(yh + 1, x + 1), far, other_far)

    def product(phase, pair, m):
        slots = pl.ds(8 * phase, 8)
        cols = pl.ds(pl.multiple_of(m * 256, 256), 256)
        lhs = xa[slots, pl.ds(2 * pair, 2), :, cols].reshape(256, 256)

        def token_rows(part):
            return ga[slots, pl.ds(pl.multiple_of(part * SUB, SUB), SUB), :]

        rhs = jnp.stack([token_rows(sources[2 * pair]), token_rows(sources[2 * pair + 1])], axis=1).reshape(256, CH)
        new = lax.dot_general(lhs, rhs, (((0,), (0,)), ((), ())), preferred_element_type=F32)
        if phase == 0 and pair == 0:
            wacc[cols, :] = new
        else:
            wacc[cols, :] += new

    pieces = frs.at[pl.ds(1, NQ - 1)]
    rs_all = remote(pieces, pieces, rs_s.at[0], rs_r.at[0], (above, ten))
    rs_all.wait_recv()
    total = fsum[pl.ds(pl.multiple_of(q * 8, 8), 8), :]
    for i in range(1, NQ):
        total = total + frs[i]
    my_rows = pl.ds(pl.multiple_of(q * 8, 8), 8)
    ffull[my_rows, mine] = total

    def fa_copy(i, source):
        ref = ffull.at[pl.ds(pl.multiple_of(source * 8, 8), 8), mine]
        return remote(ref, ref, fa_s.at[0], fa_r.at[0], (q_of(i, 1) * 2 + core, ten))

    def fa_start(i, carry):
        fa_copy(i, q).start()
        return carry

    lax.fori_loop(1, NQ, fa_start, 0)

    product(0, 0, 0)
    product(0, 0, 1)
    ag_x(0, 0, 1).wait_recv()
    product(0, 1, 0)
    product(0, 1, 1)
    ag_x(0, 1, 1).wait_recv()
    product(0, 2, 0)
    product(0, 2, 1)
    c_pass_on(2)
    c_sum_y(3)
    right(4, 0).wait_recv()
    left(4, 1).wait_recv()
    ag_far(0, 0).wait_recv()
    ag_far(0, 1).wait_recv()
    product(0, 3, 0)
    product(0, 3, 1)
    c_end(0)
    c_end(1)
    c_end(2)
    c_pass_on(3)

    product(1, 0, 0)
    product(1, 0, 1)
    ag_x(1, 0, 0).wait_recv()
    product(1, 1, 0)
    product(1, 1, 1)
    ag_x(1, 1, 0).wait_recv()
    product(1, 2, 0)
    product(1, 2, 1)
    ag_far(1, 0).wait_recv()
    ag_far(1, 1).wait_recv()
    partner_rows = pl.ds(pl.multiple_of((1 - core) * 256, 256), 256)
    product(1, 3, 1 - core)
    w_core = remote(wacc.at[partner_rows, :], wrecv, core_s.at[2], core_r.at[2], partner)
    w_core.start()
    product(1, 3, core)

    fa_all = remote(pieces, pieces, fa_s.at[0], fa_r.at[0], (above, ten))
    fa_all.wait_recv()
    f_back = remote(ffull.at[:, mine], ffull.at[:, mine], core_s.at[1], core_r.at[1], partner)
    f_back.start()
    c_end(3)
    copy = pltpu.make_async_copy(ig, ig_hbm, out_sems.at[5])
    copy.start()
    out_copies.append(copy)

    w_core.wait_recv()
    for n in range(4):
        rows = pl.ds(64 * n, 64)
        wout[rows, :] = wacc[pl.ds(pl.multiple_of(core * 256 + 64 * n, 64), 64), :] + wrecv[rows, :]
        copy = pltpu.make_async_copy(wout.at[rows, :], wg_hbm.at[rows, :], out_sems.at[6 + n])
        copy.start()
        out_copies.append(copy)

    f_back_wait = remote(ffull.at[:, theirs], ffull.at[:, theirs], core_s.at[1], core_r.at[1], partner)
    f_back_wait.wait_recv()
    fgt[...] = ffull[...].T
    sgv[...] = ffull[pl.ds(0, 1), :]
    for copy in (
        pltpu.make_async_copy(fgt, fg_hbm, out_sems.at[3]),
        pltpu.make_async_copy(sgv, sg_hbm, out_sems.at[4]),
    ):
        copy.start()
        out_copies.append(copy)

    halo_delta.wait_send()
    halo_inner.wait_send()

    slots = xa.at[pl.ds(1, NQ - 1), 0]
    remote(slots, slots, a2a_s.at[0], a2a_r.at[0], (above, ten)).wait_send()
    seven = xa.at[:, pl.ds(0, NT - 1)]
    remote(seven, seven, ag_s.at[0], ag_r.at[0], (above, ten)).wait_send()
    remote(seven, seven, c_s.at[0], c_r.at[0], (above, ten)).wait_send()
    blocks = ga.at[pl.ds(1, NQ - 1)]
    remote(blocks, blocks, b_s.at[0], b_r.at[0], (above, ten)).wait_send()
    rs_all.wait_send()
    fa_all.wait_send()
    f_core.wait_send()
    f_back.wait_send()
    w_core.wait_send()
    for copy in out_copies:
        copy.wait()


def finish(*refs):
    ins, outs, held, (in_sems, out_sems) = refs[:7], refs[7:14], refs[14:21], refs[21:]
    reads, writes = [], []
    for i, pieces in enumerate(PIECES):
        rows = ins[i].shape[0] // pieces
        for n in range(pieces):
            part = pl.ds(rows * n, rows)
            at = len(reads)
            reads.append(pltpu.make_async_copy(ins[i].at[part, :], held[i].at[part, :], in_sems.at[at]))
            writes.append(pltpu.make_async_copy(held[i].at[part, :], outs[i].at[part, :], out_sems.at[at]))
    for read in reads:
        read.start()
    for read, write in zip(reads, writes):
        read.wait()
        write.start()
    for write in writes:
        write.wait()


def local(layer_input, query_stream, key_stream, value_stream, output_grad, filter_taps, skip_gain, value_weight):
    shape = jax.ShapeDtypeStruct
    vm = pltpu.VMEM
    dma = pltpu.SemaphoreType.DMA
    outs = pl.pallas_call(
        kernel,
        out_shape=(
            shape((ROWS, CH), BF16),
            shape((ROWS, CH), BF16),
            shape((ROWS, CH), BF16),
            shape((CH, TAPS), F32),
            shape((1, CH), F32),
            shape((SUB, D), BF16),
            shape((256, CH), F32),
        ),
        in_specs=[pl.BlockSpec(memory_space=pl.ANY)] * 8,
        out_specs=[pl.BlockSpec(memory_space=pl.ANY)] * 7,
        scratch_shapes=[
            vm((ROWS, CH), BF16),
            vm((ROWS, CH), BF16),
            vm((ROWS, CH), BF16),
            vm((ROWS, CH), BF16),
            vm((CH, TAPS), BF16),
            vm((1, CH), F32),
            vm((SUB, D), BF16),
            vm((D, CH), BF16),
            vm((ROWS, CH), BF16),
            vm((ROWS, CH), BF16),
            vm((ROWS, CH), BF16),
            vm((ROWS, CH), BF16),
            vm((TAPS, CH), F32),
            vm((2 * ROWS, CH), F32),
            vm((2 * ROWS, CH), F32),
            vm((8, 32, 8, CH), F32),
            vm((8, 32, 8, CH), F32),
            vm((16, 8, CH), F32),
            vm((16, 8, CH), F32),
            vm((ROWS, CH), BF16),
            vm((ROWS, CH), BF16),
            vm((NQ, NT, SUB, WIDE), BF16),
            vm((NQ, ROWS, CH), BF16),
            vm((NYH, NX, SUB, D), BF16),
            vm((NX, SUB, D), BF16),
            vm((NYH, NX, SUB, D), BF16),
            vm((CHUNKS, NYH, SUB, CCOLS), BF16),
            vm((CHUNKS, NYH, SUB, CCOLS), BF16),
            vm((CHUNKS, NYH, SUB, CCOLS), BF16),
            vm((CHUNKS, NYH, SUB, CCOLS), BF16),
            vm((SUB, D), BF16),
            vm((SUB, D), F32),
            vm((SUB, D), BF16),
            vm((WIDE, CH), F32),
            vm((256, CH), F32),
            vm((256, CH), F32),
            vm((TAPS, CH), F32),
            vm((TAPS, CH // 2), F32),
            vm((TAPS, CH // 2), F32),
            vm((NQ, 8, CH // 2), F32),
            vm((TAPS, CH), F32),
            vm((CH, TAPS), F32),
            vm((1, CH), F32),
            dma((9,)),
            dma((10,)),
            dma((2,)), dma((2,)),
            dma((1,)), dma((2,)),
            dma((1,)), dma((14,)),
            dma((1,)), dma((17,)),
            dma((1,)), dma((8 * CHUNKS,)),
            dma((3,)), dma((3,)),
            dma((1,)), dma((1,)),
            dma((1,)), dma((1,)),
        ],
        compiler_params=pltpu.CompilerParams(
            collective_id=0, has_side_effects=True, vmem_limit_bytes=VMEM_LIMIT
        ),
        name="hyena_back",
    )(
        layer_input, query_stream, key_stream, value_stream, output_grad, filter_taps,
        skip_gain.reshape(1, CH), value_weight,
    )
    outs = pl.pallas_call(
        finish,
        out_shape=tuple(shape(out.shape, out.dtype) for out in outs),
        in_specs=[pl.BlockSpec(memory_space=pl.ANY)] * 7,
        out_specs=[pl.BlockSpec(memory_space=pl.ANY)] * 7,
        scratch_shapes=[vm(out.shape, out.dtype) for out in outs] + [dma((sum(PIECES),)), dma((sum(PIECES),))],
        compiler_params=pltpu.CompilerParams(vmem_limit_bytes=VMEM_LIMIT),
        name="finish",
    )(*outs)
    query_grad, key_grad, value_grad, filter_grad, skip_grad, input_grad, weight_grad = outs
    return (query_grad, key_grad, value_grad, filter_grad, skip_grad.reshape(CH), input_grad, weight_grad)


def solution(mesh):
    placed = (
        P(("context", "tensor"), None),
        P("context", "tensor"),
        P("context", "tensor"),
        P("context", "tensor"),
        P("context", "tensor"),
        P("tensor", None),
        P("tensor"),
        P(None, "tensor"),
    )
    return jax.shard_map(
        local,
        mesh=mesh,
        in_specs=placed,
        out_specs=(
            P("context", "tensor"),
            P("context", "tensor"),
            P("context", "tensor"),
            P("tensor", None),
            P("tensor"),
            P(("context", "tensor"), None),
            P("context", "tensor"),
        ),
        check_vma=False,
    )
```

```python
import jax
import jax.numpy as jnp
from jax import lax
from jax.experimental import pallas as pl
from jax.experimental.pallas import tpu as pltpu
from jax.sharding import PartitionSpec as P

MESH = pl.DeviceIdType.MESH
BF16 = jnp.bfloat16
F32 = jnp.float32

NZ, NYL, NCORE, NYH, NX = 8, 2, 2, 2, 4
NQ = NZ * NYL
NT = NYH * NX
TAPS = 128
ROWS = 128
CH = 512
SUB = 16
D = 8192
WIDE = D // NQ
CHUNKS = 4
CCOLS = D // CHUNKS
X_FIRST = (0,)
ORDER = (0, 1, 7, 2, 6, 3, 5, 4)
VMEM_LIMIT = 63 << 20
PIECES = (1, 1, 1, 2, 1, 1, 4)


def kernel(
    x_hbm, q_hbm, k_hbm, v_hbm, g_hbm, taps_hbm, gain_hbm, w_hbm,
    qg_hbm, kg_hbm, vg_hbm, fg_hbm, sg_hbm, ig_hbm, wg_hbm,
    qv, kv, vv, gv, taps_v, gain_v, x_v, w_v,
    inner, delta, halo_d, halo_i, tapst, dext, iext, d8, e8, back, mix,
    qgv, kgv, xa, ga, tpart, yr, sums, from_left, from_right, left_sum, right_sum, ysend, isum, ig, wacc, wrecv, wout,
    fpart, fcore, fsum, frs, ffull, fgt, sgv,
    in_sems, out_sems, halo_s, halo_r, a2a_s, a2a_r, ag_s, ag_r, b_s, b_r, c_s, c_r,
    core_s, core_r, rs_s, rs_r, fa_s, fa_r,
):
    con = lax.axis_index("context")
    ten = lax.axis_index("tensor")
    z, yl, core = con // 4, (con // 2) % 2, con % 2
    yh, x = ten // 4, ten % 4
    q = con // 2

    def at(zz, yy, cc):
        return (zz % NZ) * 4 + (yy % 2) * 2 + cc % 2

    def ten_at(hh, xx):
        return (hh % 2) * 4 + xx % 4

    def remote(src, dst, ss, rs, device):
        return pltpu.make_async_remote_copy(
            src_ref=src, dst_ref=dst, send_sem=ss, recv_sem=rs, device_id=device, device_id_type=MESH
        )

    loads = [
        pltpu.make_async_copy(src, dst, in_sems.at[i])
        for i, (src, dst) in enumerate(
            [(k_hbm, kv), (v_hbm, vv), (g_hbm, gv), (q_hbm, qv), (taps_hbm, taps_v), (gain_hbm, gain_v), (x_hbm, x_v), (w_hbm, w_v)]
        )
    ]
    barrier = pltpu.get_barrier_semaphore()
    above = (con + 1) % 32
    below = (con + 31) % 32

    def greet(device):
        pl.semaphore_signal(barrier, inc=1, device_id=device, device_id_type=MESH)

    for dz in (4, 3, 5, 2, 6, 1, 7, 0):
        for dy in range(2):
            if (dz, dy) != (0, 0):
                greet((at(z + dz, yl + dy, core), ten))
    for i in (6, 2, 5, 7, 4, 1, 3):
        greet((con, (ten + i) % NT))
    greet((above, ten))
    greet((below, ten))
    greet((at(z, yl, core + 1), ten))
    for copy in loads:
        copy.start()


    loads[0].wait()
    loads[1].wait()
    loads[2].wait()
    loads[3].wait()
    inner[...] = (kv[...].astype(F32) * vv[...].astype(F32)).astype(BF16)
    delta[...] = (gv[...].astype(F32) * qv[...].astype(F32)).astype(BF16)
    pl.semaphore_wait(barrier, 3 + (NQ - 1) + (NT - 1))

    halo_delta = remote(delta, halo_d, halo_s.at[0], halo_r.at[0], (below, ten))
    halo_inner = remote(inner, halo_i, halo_s.at[1], halo_r.at[1], (above, ten))
    halo_delta.start()

    own_x = pltpu.make_async_copy(
        x_v.at[:, pl.ds(pl.multiple_of(q * WIDE, WIDE), WIDE)], xa.at[0, 0], in_sems.at[8]
    )
    loads[6].wait()
    own_x.start()

    def a2a_copy(slot):
        dest = ((z + ORDER[slot // 2]) % NZ) * 2 + (yl + slot % 2) % 2
        return remote(
            x_v.at[:, pl.ds(pl.multiple_of(dest * WIDE, WIDE), WIDE)],
            xa.at[slot, 0],
            a2a_s.at[0],
            a2a_r.at[slot // 8],
            (dest * 2 + core, ten),
        )

    for slot in (14, 15, 10, 11, 12, 13, 6, 7, 8, 9, 2, 3, 4, 5, 1):
        a2a_copy(slot).start()
    halo_inner.start()

    dext[pl.ds(0, ROWS), :] = delta[...].astype(F32)
    iext[pl.ds(ROWS, ROWS), :] = inner[...].astype(F32)

    loads[4].wait()
    loads[5].wait()
    tapst[...] = taps_v[...].astype(F32).T

    for r in range(8):
        d8[r, pl.ds(0, 15)] = dext[pl.ds(r, 120), :].reshape(15, 8, CH)

    def lanes(l):
        return pl.ds(pl.multiple_of(l * 128, 128), 128)

    def tap_row(j, cols):
        return jnp.broadcast_to(tapst[pl.ds(j, 1), cols], (8, 128))

    def chain(taps, tiles):
        total = taps[0] * tiles[0]
        for tap, tile in zip(taps[1:], tiles[1:]):
            total = total + tap * tile
        return total

    def back_own(l, carry):
        cols = lanes(l)
        gain = jnp.broadcast_to(gain_v[:, cols], (8, 128))
        for r in range(8):
            tiles = [d8[r, k, :, cols] for k in range(15)]
            taps = [tap_row(8 * a + r, cols) for a in range(15)]
            for i in range(15):
                total = chain(taps[: 15 - i], tiles[i:])
                back[i, :, cols] = total + gain * tiles[i] if r == 0 else back[i, :, cols] + total
        back[15, :, cols] = gain * dext[pl.ds(120, 8), cols]
        return carry

    def back_halo(l, carry):
        cols = lanes(l)
        for r in range(8):
            tiles = [d8[r, 15 + k, :, cols] for k in range(16)]
            taps = [tap_row(8 * a + r, cols) for a in range(16)]
            for i in range(16):
                back[i, :, cols] = back[i, :, cols] + chain(taps[15 - i :], tiles[: i + 1])
        return carry

    lax.fori_loop(0, 4, back_own, 0)

    x_up, x_down = ten_at(yh, x + 1), ten_at(yh, x + 3)
    other = ten_at(yh + 1, x)

    def ag_copy(index, phase, source, target, device):
        slots = pl.ds(8 * phase, 8)
        return remote(xa.at[slots, source], xa.at[slots, target], ag_s.at[0], ag_r.at[index], (con, device))

    def ag_y(phase):
        return ag_copy(phase, phase, 0, 1, other)

    def ag_x(phase, row, way):
        index = 2 + phase * 4 + row * 2 + way
        return ag_copy(index, phase, row, 2 + 2 * row + way, x_down if way else x_up)

    def ag_far(phase, row):
        index = 10 + phase * 2 + row
        return ag_copy(index, phase, 2 + 2 * row + phase, 6 + row, x_down if phase else x_up)

    def ag_own(phase):
        if phase == 0:
            own_x.wait()
        group = xa.at[pl.ds(8, 8), 0] if phase else xa.at[pl.ds(1, 7), 0]
        remote(group, group, a2a_s.at[0], a2a_r.at[phase], (above, ten)).wait_recv()
        ag_y(phase).start()
        ag_x(phase, 0, 0).start()
        ag_x(phase, 0, 1).start()

    def ag_other(phase):
        ag_y(phase).wait_recv()
        ag_x(phase, 1, 0).start()
        ag_x(phase, 1, 1).start()

    def ag_forward(phase, row):
        ag_x(phase, row, phase).wait_recv()
        ag_far(phase, row).start()


    halo_delta.wait_recv()
    keep_d = jnp.where(con == 31, 0.0, 1.0).astype(F32)
    dext[pl.ds(ROWS, ROWS), :] = halo_d[...].astype(F32) * keep_d
    for r in range(8):
        d8[r, pl.ds(15, 16)] = dext[pl.ds(120 + r, ROWS), :].reshape(16, 8, CH)
    lax.fori_loop(0, 4, back_halo, 0)

    backs = back[...].reshape(ROWS, CH)
    ga[0] = (backs * kv[...].astype(F32)).astype(BF16)

    def b_copy(index, source, target, device):
        return remote(ga.at[source], ga.at[target], b_s.at[0], b_r.at[index], (device, ten))

    up, down = at(z + 1, yl, core), at(z + 7, yl, core)

    def slot_of(dz, rel):
        return 2 * ORDER.index(dz % NZ) + rel

    def right(d, rel):
        return b_copy(1 + (d - 1) * 4 + rel, slot_of(d - 1, rel), slot_of(d, rel), up)

    def left(d, rel):
        return b_copy(1 + (d - 1) * 4 + 2 + rel, slot_of(1 - d, rel), slot_of(-d, rel), down)

    def forward(d, rel):
        right(d, rel).wait_recv()
        if d < 3 or rel == 0:
            right(d + 1, rel).start()
        left(d, rel).wait_recv()
        if d < 3 or rel == 1:
            left(d + 1, rel).start()

    right(1, 0).start()
    left(1, 0).start()
    across = b_copy(0, 0, 1, at(z, yl + 1, core))
    across.start()


    loads[7].wait()

    ccols = [pl.ds(chunk * CCOLS, CCOLS) for chunk in range(CHUNKS)]
    first_half = [pl.ds(chunk * CCOLS, CCOLS // 2) for chunk in range(CHUNKS)]
    second_half = [pl.ds(chunk * CCOLS + CCOLS // 2, CCOLS // 2) for chunk in range(CHUNKS)]
    lo, hi = pl.ds(0, CCOLS // 2), pl.ds(CCOLS // 2, CCOLS // 2)
    hops = [(x + dx) % 4 for dx in range(4)]

    def c_remote(chunk, kind, src, dst, device):
        index = chunk * 8 + kind
        return remote(src, dst, c_s.at[0], c_r.at[index], (con, device))

    def y_copy(chunk):
        return c_remote(chunk, 0, tpart.at[1 - yh, :, :, ccols[chunk]], yr.at[:, :, ccols[chunk]], other)

    def x_refs(chunk, dx, part):
        if chunk in X_FIRST:
            return tpart.at[:, hops[dx], :, part[chunk]]
        return sums.at[pl.ds(0, 1), dx, :, part[chunk]]

    def groups(chunk):
        return pl.ds(0, 2) if chunk in X_FIRST else pl.ds(0, 1)

    def x_copy(chunk, kind):
        g = groups(chunk)
        src, dst, device = (
            (x_refs(chunk, 2, first_half), from_left.at[chunk, g, :, lo], x_up),
            (x_refs(chunk, 2, second_half), from_right.at[chunk, g, :, hi], x_down),
            (x_refs(chunk, 1, second_half), left_sum.at[chunk, g, :, hi], x_up),
            (x_refs(chunk, 3, first_half), right_sum.at[chunk, g, :, lo], x_down),
            (sums.at[g, 1, :, first_half[chunk]], left_sum.at[chunk, g, :, lo], x_up),
            (sums.at[g, 3, :, second_half[chunk]], right_sum.at[chunk, g, :, hi], x_down),
        )[kind]
        return c_remote(chunk, 1 + kind, src, dst, device)

    def yx_copy(chunk):
        return c_remote(chunk, 7, ysend.at[:, ccols[chunk]], yr.at[0, :, ccols[chunk]], other)

    def f32(ref, *index):
        return ref[index].astype(F32)

    def terms(chunk):
        def part(n, carry):
            cols = pl.ds(pl.multiple_of(chunk * CCOLS + n * 512, 512), 512)
            product = lax.dot_general(ga[0], w_v[cols, :], (((1,), (1,)), ((), ())), preferred_element_type=F32)
            tpart[:, :, :, cols] = product.astype(BF16).reshape(NYH, NX, SUB, 512)
            return carry

        lax.fori_loop(0, CCOLS // 512, part, 0)
        if chunk in X_FIRST:
            for kind in range(4):
                x_copy(chunk, kind).start()
        else:
            y_copy(chunk).start()

    def c_sum_y(chunk):
        y_copy(chunk).wait_recv()
        for dx in (2, 1, 3):
            total = f32(tpart, yh, hops[dx], slice(None), ccols[chunk]) + f32(yr, hops[dx], slice(None), ccols[chunk])
            sums[0, dx, :, ccols[chunk]] = total.astype(BF16)
        for kind in range(4):
            x_copy(chunk, kind).start()

    def c_pass_on(chunk):
        g = groups(chunk)
        for kind, dx, part, here, arrived in ((0, 1, first_half, lo, from_left), (1, 3, second_half, hi, from_right)):
            x_copy(chunk, kind).wait_recv()
            mine = x_refs(chunk, dx, part)[...].astype(F32)
            sums[g, dx, :, part[chunk]] = (mine + f32(arrived, chunk, g, slice(None), here)).astype(BF16)
            x_copy(chunk, kind + 4).start()

    def c_wait_x(chunk):
        for kind in range(2, 6):
            x_copy(chunk, kind).wait_recv()

    def c_turn_y(chunk):
        c_wait_x(chunk)
        cols = ccols[chunk]

        def total(h):
            return f32(tpart, h, x, slice(None), cols) + f32(left_sum, chunk, h) + f32(right_sum, chunk, h)

        ysend[:, cols] = total(1 - yh).astype(BF16)
        yx_copy(chunk).start()
        isum[:, cols] = total(yh)

    def c_end(chunk):
        cols = ccols[chunk]
        if chunk in X_FIRST:
            yx_copy(chunk).wait_recv()
            ig[:, cols] = (isum[:, cols] + f32(yr, 0, slice(None), cols)).astype(BF16)
        else:
            c_wait_x(chunk)
            total = f32(tpart, yh, x, slice(None), cols) + f32(yr, x, slice(None), cols)
            ig[:, cols] = (total + f32(left_sum, chunk, 0) + f32(right_sum, chunk, 0)).astype(BF16)

    def filter_tile(l, carry):
        cols = lanes(l)
        rows = [iext[pl.ds(ROWS + 8 * i, 8), cols] for i in range(16)]
        for r in range(8):
            tiles = [d8[r, k, :, cols] for k in range(31)]
            for a in range(16):
                total = rows[0] * tiles[a]
                for i in range(1, 16):
                    total = total + rows[i] * tiles[i + a]
                fpart[pl.ds(8 * a + r, 1), cols] = jnp.sum(total, axis=0, keepdims=True)
        return carry

    ag_own(0)
    terms(0)
    ag_own(1)
    forward(1, 0)
    across.wait_recv()
    right(1, 1).start()
    left(1, 1).start()
    terms(1)
    lax.fori_loop(0, 2, filter_tile, 0)
    ag_other(0)
    forward(2, 0)
    ag_forward(0, 0)
    lax.fori_loop(2, 4, filter_tile, 0)

    half = CH // 2
    mine = pl.ds(pl.multiple_of(core * half, half), half)
    theirs = pl.ds(pl.multiple_of((1 - core) * half, half), half)
    partner = (at(z, yl, core + 1), ten)
    f_core = remote(fpart.at[:, theirs], fcore, core_s.at[0], core_r.at[0], partner)
    f_core.start()
    forward(1, 1)
    ag_other(1)
    terms(2)

    f_core.wait_recv()
    fsum[...] = fpart[:, mine] + fcore[...]

    def q_of(i, way):
        return ((z + NZ + way * (i // 2)) % NZ) * 2 + (yl + i % 2) % 2

    def rs_copy(i):
        dest = q_of(i, 1)
        return remote(
            fsum.at[pl.ds(pl.multiple_of(dest * 8, 8), 8), :], frs.at[i], rs_s.at[0], rs_r.at[0], (dest * 2 + core, ten)
        )

    def rs_start(i, carry):
        rs_copy(i).start()
        return carry

    lax.fori_loop(1, NQ, rs_start, 0)
    forward(3, 0)
    c_pass_on(0)
    ag_forward(1, 0)
    ag_forward(0, 1)
    terms(3)
    forward(2, 1)

    kgv[...] = (back[...].reshape(ROWS, CH) * vv[...].astype(F32)).astype(BF16)
    out_copies = [
        pltpu.make_async_copy(kgv, kg_hbm, out_sems.at[0]),
        pltpu.make_async_copy(ga.at[0], vg_hbm, out_sems.at[1]),
    ]
    for copy in out_copies:
        copy.start()


    halo_inner.wait_recv()
    keep_i = jnp.where(con == 0, 0.0, 1.0).astype(F32)
    iext[pl.ds(0, ROWS), :] = halo_i[...].astype(F32) * keep_i
    e8[0] = iext[...].reshape(32, 8, CH)
    for r in range(1, 8):
        e8[r, pl.ds(0, 31)] = iext[pl.ds(r, 248), :].reshape(31, 8, CH)

    def mixed_tile(l, carry):
        cols = lanes(l)
        gain = jnp.broadcast_to(gain_v[:, cols], (8, 128))
        for r in range(8):
            skip = 1 if r == 0 else 0
            taps = [tap_row(TAPS - 8 * (b + skip) - r, cols) for b in range(16)]
            for start in (0, 8):
                tiles = [e8[r, start + k + skip, :, cols] for k in range(23)]
                for i in range(8):
                    total = chain(taps, tiles[i : i + 16])
                    at_i = (start + i, slice(None), cols)
                    mix[at_i] = total + gain * tiles[i + 15] if r == 0 else mix[at_i] + total
        mixed = mix[:, :, cols].reshape(ROWS, 128)
        qgv[:, cols] = (gv[:, cols].astype(F32) * mixed).astype(BF16)
        return carry

    c_sum_y(1)
    lax.fori_loop(0, 2, mixed_tile, 0)
    ag_forward(1, 1)
    c_pass_on(1)
    lax.fori_loop(2, 4, mixed_tile, 0)
    copy = pltpu.make_async_copy(qgv, qg_hbm, out_sems.at[2])
    copy.start()
    out_copies.append(copy)

    forward(3, 1)
    if 0 in X_FIRST:
        c_turn_y(0)
    c_sum_y(2)

    far, other_far = ten_at(yh, x + 2), ten_at(yh + 1, x + 2)
    sources = (ten, other, x_down, x_up, ten_at(yh + 1, x + 3), ten_at(yh + 1, x + 1), far, other_far)

    def product(phase, pair, m):
        slots = pl.ds(8 * phase, 8)
        cols = pl.ds(pl.multiple_of(m * 256, 256), 256)
        lhs = xa[slots, pl.ds(2 * pair, 2), :, cols].reshape(256, 256)

        def token_rows(part):
            return ga[slots, pl.ds(pl.multiple_of(part * SUB, SUB), SUB), :]

        rhs = jnp.stack([token_rows(sources[2 * pair]), token_rows(sources[2 * pair + 1])], axis=1).reshape(256, CH)
        new = lax.dot_general(lhs, rhs, (((0,), (0,)), ((), ())), preferred_element_type=F32)
        if phase == 0 and pair == 0:
            wacc[cols, :] = new
        else:
            wacc[cols, :] += new

    pieces = frs.at[pl.ds(1, NQ - 1)]
    rs_all = remote(pieces, pieces, rs_s.at[0], rs_r.at[0], (above, ten))
    rs_all.wait_recv()
    total = fsum[pl.ds(pl.multiple_of(q * 8, 8), 8), :]
    for i in range(1, NQ):
        total = total + frs[i]
    my_rows = pl.ds(pl.multiple_of(q * 8, 8), 8)
    ffull[my_rows, mine] = total

    def fa_copy(i, source):
        ref = ffull.at[pl.ds(pl.multiple_of(source * 8, 8), 8), mine]
        return remote(ref, ref, fa_s.at[0], fa_r.at[0], (q_of(i, 1) * 2 + core, ten))

    def fa_start(i, carry):
        fa_copy(i, q).start()
        return carry

    lax.fori_loop(1, NQ, fa_start, 0)

    product(0, 0, 0)
    product(0, 0, 1)
    ag_x(0, 0, 1).wait_recv()
    product(0, 1, 0)
    product(0, 1, 1)
    ag_x(0, 1, 1).wait_recv()
    product(0, 2, 0)
    product(0, 2, 1)
    c_pass_on(2)
    c_sum_y(3)
    right(4, 0).wait_recv()
    left(4, 1).wait_recv()
    ag_far(0, 0).wait_recv()
    ag_far(0, 1).wait_recv()
    product(0, 3, 0)
    product(0, 3, 1)
    c_end(0)
    c_end(1)
    c_end(2)
    c_pass_on(3)

    product(1, 0, 0)
    product(1, 0, 1)
    ag_x(1, 0, 0).wait_recv()
    product(1, 1, 0)
    product(1, 1, 1)
    ag_x(1, 1, 0).wait_recv()
    product(1, 2, 0)
    product(1, 2, 1)
    ag_far(1, 0).wait_recv()
    ag_far(1, 1).wait_recv()
    partner_rows = pl.ds(pl.multiple_of((1 - core) * 256, 256), 256)
    product(1, 3, 1 - core)
    w_core = remote(wacc.at[partner_rows, :], wrecv, core_s.at[2], core_r.at[2], partner)
    w_core.start()
    product(1, 3, core)

    fa_all = remote(pieces, pieces, fa_s.at[0], fa_r.at[0], (above, ten))
    fa_all.wait_recv()
    f_back = remote(ffull.at[:, mine], ffull.at[:, mine], core_s.at[1], core_r.at[1], partner)
    f_back.start()
    c_end(3)
    copy = pltpu.make_async_copy(ig, ig_hbm, out_sems.at[5])
    copy.start()
    out_copies.append(copy)

    w_core.wait_recv()
    for n in range(4):
        rows = pl.ds(64 * n, 64)
        wout[rows, :] = wacc[pl.ds(pl.multiple_of(core * 256 + 64 * n, 64), 64), :] + wrecv[rows, :]
        copy = pltpu.make_async_copy(wout.at[rows, :], wg_hbm.at[rows, :], out_sems.at[6 + n])
        copy.start()
        out_copies.append(copy)

    f_back_wait = remote(ffull.at[:, theirs], ffull.at[:, theirs], core_s.at[1], core_r.at[1], partner)
    f_back_wait.wait_recv()
    fgt[...] = ffull[...].T
    sgv[...] = ffull[pl.ds(0, 1), :]
    for copy in (
        pltpu.make_async_copy(fgt, fg_hbm, out_sems.at[3]),
        pltpu.make_async_copy(sgv, sg_hbm, out_sems.at[4]),
    ):
        copy.start()
        out_copies.append(copy)

    halo_delta.wait_send()
    halo_inner.wait_send()

    slots = xa.at[pl.ds(1, NQ - 1), 0]
    remote(slots, slots, a2a_s.at[0], a2a_r.at[0], (above, ten)).wait_send()
    seven = xa.at[:, pl.ds(0, NT - 1)]
    remote(seven, seven, ag_s.at[0], ag_r.at[0], (above, ten)).wait_send()
    remote(seven, seven, c_s.at[0], c_r.at[0], (above, ten)).wait_send()
    blocks = ga.at[pl.ds(1, NQ - 1)]
    remote(blocks, blocks, b_s.at[0], b_r.at[0], (above, ten)).wait_send()
    rs_all.wait_send()
    fa_all.wait_send()
    f_core.wait_send()
    f_back.wait_send()
    w_core.wait_send()
    for copy in out_copies:
        copy.wait()


def finish(*refs):
    ins, outs, held, (in_sems, out_sems) = refs[:7], refs[7:14], refs[14:21], refs[21:]
    reads, writes = [], []
    for i, pieces in enumerate(PIECES):
        rows = ins[i].shape[0] // pieces
        for n in range(pieces):
            part = pl.ds(rows * n, rows)
            at = len(reads)
            reads.append(pltpu.make_async_copy(ins[i].at[part, :], held[i].at[part, :], in_sems.at[at]))
            writes.append(pltpu.make_async_copy(held[i].at[part, :], outs[i].at[part, :], out_sems.at[at]))
    for read in reads:
        read.start()
    for read, write in zip(reads, writes):
        read.wait()
        write.start()
    for write in writes:
        write.wait()


def local(layer_input, query_stream, key_stream, value_stream, output_grad, filter_taps, skip_gain, value_weight):
    shape = jax.ShapeDtypeStruct
    vm = pltpu.VMEM
    dma = pltpu.SemaphoreType.DMA
    outs = pl.pallas_call(
        kernel,
        out_shape=(
            shape((ROWS, CH), BF16),
            shape((ROWS, CH), BF16),
            shape((ROWS, CH), BF16),
            shape((CH, TAPS), F32),
            shape((1, CH), F32),
            shape((SUB, D), BF16),
            shape((256, CH), F32),
        ),
        in_specs=[pl.BlockSpec(memory_space=pl.ANY)] * 8,
        out_specs=[pl.BlockSpec(memory_space=pl.ANY)] * 7,
        scratch_shapes=[
            vm((ROWS, CH), BF16),
            vm((ROWS, CH), BF16),
            vm((ROWS, CH), BF16),
            vm((ROWS, CH), BF16),
            vm((CH, TAPS), BF16),
            vm((1, CH), F32),
            vm((SUB, D), BF16),
            vm((D, CH), BF16),
            vm((ROWS, CH), BF16),
            vm((ROWS, CH), BF16),
            vm((ROWS, CH), BF16),
            vm((ROWS, CH), BF16),
            vm((TAPS, CH), F32),
            vm((2 * ROWS, CH), F32),
            vm((2 * ROWS, CH), F32),
            vm((8, 32, 8, CH), F32),
            vm((8, 32, 8, CH), F32),
            vm((16, 8, CH), F32),
            vm((16, 8, CH), F32),
            vm((ROWS, CH), BF16),
            vm((ROWS, CH), BF16),
            vm((NQ, NT, SUB, WIDE), BF16),
            vm((NQ, ROWS, CH), BF16),
            vm((NYH, NX, SUB, D), BF16),
            vm((NX, SUB, D), BF16),
            vm((NYH, NX, SUB, D), BF16),
            vm((CHUNKS, NYH, SUB, CCOLS), BF16),
            vm((CHUNKS, NYH, SUB, CCOLS), BF16),
            vm((CHUNKS, NYH, SUB, CCOLS), BF16),
            vm((CHUNKS, NYH, SUB, CCOLS), BF16),
            vm((SUB, D), BF16),
            vm((SUB, D), F32),
            vm((SUB, D), BF16),
            vm((WIDE, CH), F32),
            vm((256, CH), F32),
            vm((256, CH), F32),
            vm((TAPS, CH), F32),
            vm((TAPS, CH // 2), F32),
            vm((TAPS, CH // 2), F32),
            vm((NQ, 8, CH // 2), F32),
            vm((TAPS, CH), F32),
            vm((CH, TAPS), F32),
            vm((1, CH), F32),
            dma((9,)),
            dma((10,)),
            dma((2,)), dma((2,)),
            dma((1,)), dma((2,)),
            dma((1,)), dma((14,)),
            dma((1,)), dma((17,)),
            dma((1,)), dma((8 * CHUNKS,)),
            dma((3,)), dma((3,)),
            dma((1,)), dma((1,)),
            dma((1,)), dma((1,)),
        ],
        compiler_params=pltpu.CompilerParams(
            collective_id=0, has_side_effects=True, vmem_limit_bytes=VMEM_LIMIT
        ),
        name="hyena_back",
    )(
        layer_input, query_stream, key_stream, value_stream, output_grad, filter_taps,
        skip_gain.reshape(1, CH), value_weight,
    )
    outs = pl.pallas_call(
        finish,
        out_shape=tuple(shape(out.shape, out.dtype) for out in outs),
        in_specs=[pl.BlockSpec(memory_space=pl.ANY)] * 7,
        out_specs=[pl.BlockSpec(memory_space=pl.ANY)] * 7,
        scratch_shapes=[vm(out.shape, out.dtype) for out in outs] + [dma((sum(PIECES),)), dma((sum(PIECES),))],
        compiler_params=pltpu.CompilerParams(vmem_limit_bytes=VMEM_LIMIT),
        name="finish",
    )(*outs)
    query_grad, key_grad, value_grad, filter_grad, skip_grad, input_grad, weight_grad = outs
    return (query_grad, key_grad, value_grad, filter_grad, skip_grad.reshape(CH), input_grad, weight_grad)


def solution(mesh):
    placed = (
        P(("context", "tensor"), None),
        P("context", "tensor"),
        P("context", "tensor"),
        P("context", "tensor"),
        P("context", "tensor"),
        P("tensor", None),
        P("tensor"),
        P(None, "tensor"),
    )
    return jax.shard_map(
        local,
        mesh=mesh,
        in_specs=placed,
        out_specs=(
            P("context", "tensor"),
            P("context", "tensor"),
            P("context", "tensor"),
            P("tensor", None),
            P("tensor"),
            P(("context", "tensor"), None),
            P("context", "tensor"),
        ),
        check_vma=False,
    )
```
